32 devices in a mesh: tm: 8 (over z, core), fsdp: 4 (over y, x).
Axes of the slice: x: 2, y: 2, z: 4, core: 2. Of those that a mesh axis runs over, the one named last changes fastest.
Arguments:
- queries: bfloat16 [4, 1024, 768], P('fsdp', 'tm'), may hold values from -135 to 135, as said below
- keys_values: bfloat16 [4, 1024, 1536], P('fsdp', 'tm'), may hold values from -4.5 to 4.5
- inputs: bfloat16 [4, 1024, 1536], P('fsdp', 'tm'), may hold values from -6 to 6
- cotangent: bfloat16 [4, 1024, 1536], P('fsdp', 'tm'), may hold values from -6 to 6
- out_weight: bfloat16 [768, 1536], P('fsdp'), may hold values from -0.21875 to 0.21875
- conv_kernel: bfloat16 [32, 1536], P(None, 'fsdp'), may hold values from -1 to 1
- utt_starts: int32 [4, 16], P('fsdp'), may hold values from 0 to 1023, as said below
Outputs:
- context_grad: bfloat16 [4, 1024, 768], P('fsdp', 'tm')
- weight_grad: float32 [768, 1536], P('fsdp')
- kernel_grad: float32 [32, 1536], P(None, 'fsdp')
The draws below stay inside these ranges and needn't reach their ends.
Inputs may be any that keep to these rules, and one draw needn't show every extreme that they name: In the hidden draw some frames' queries are large multiples of their own keys, so that a few scores are far above the rest. `utt_starts`: each row begins with 0 and rises strictly; entry u is the first frame of utterance u of that packed sequence.
All inputs are finite; a program needn't handle non-finite values.
Results may differ from the reference program's by a relative error of at most 0.014.
Values may be sent and summed in bfloat16 or wider, within the bound.
A program may use at most 128 MiB of HBM per device.

```python
import math
import jax
import jax.numpy as jnp
from jax import lax

D = 1536
HEADS_W = 8
HD = 96
KW = 32
WIN = 128
UTTS = 16
HW = 768
SEQS = 4
FRAMES = 1024


def attention_pair(key):
    base_key = jax.random.fold_in(key, 11)
    query_key, keyrow_key, value_key = jax.random.split(base_key, 3)
    draw_shape = (SEQS, FRAMES, HW)
    key_draw = jnp.clip(jax.random.normal(keyrow_key, draw_shape, jnp.float32), -4.0, 4.0)
    value_draw = jnp.clip(jax.random.normal(value_key, draw_shape, jnp.float32), -4.0, 4.0)
    query_draw = jnp.clip(jax.random.normal(query_key, draw_shape, jnp.float32), -4.0, 4.0)
    return (query_draw, jnp.concatenate([key_draw, value_draw], axis=2))


def draw_queries(key, part):
    return attention_pair(key)[0].astype(jnp.bfloat16)


def draw_keys_values(key, part):
    return attention_pair(key)[1].astype(jnp.bfloat16)


def draw_utt_starts(key, part):
    base_key = jax.random.fold_in(key, 5)
    row_keys = jax.random.split(base_key, SEQS)

    def one_row(row_key):
        chosen = jax.random.permutation(row_key, FRAMES - 2)[:UTTS - 2] + 1
        inner = jnp.sort(chosen).astype(jnp.int32)
        return jnp.concatenate([jnp.zeros((1,), jnp.int32), inner, jnp.full((1,), FRAMES - 1, jnp.int32)])
    return jax.vmap(one_row)(row_keys)


def level_of(key, dims, cuts, least, top_value):
    level, own = 1.0, jax.random.fold_in(key, 6)
    for position, shards_of in cuts:
        steps = jnp.exp(jax.random.uniform(jax.random.fold_in(own, position), (shards_of,), jnp.float32, least / len(cuts), top_value / len(cuts)))
        level = level * jnp.repeat(steps, dims[position] // shards_of).reshape([-1 if axis == position else 1 for axis in range(len(dims))])
    return level


def normal_values(key, extent, spread, most, cuts=(), kind=jnp.bfloat16):
    loudness = level_of(key, extent, cuts, -0.22, 0.18) if cuts else 1.0
    entries = jax.random.normal(key, extent, jnp.float32) * spread * loudness
    return jnp.minimum(jnp.maximum(entries, -most), most).astype(kind)


def setup_inputs(seed: int = 0) -> dict:
    seeds = jax.random.split(jax.random.key(seed), 8)
    queries = draw_queries(jax.random.fold_in(seeds[7], 71), 0)
    keys_values = draw_keys_values(jax.random.fold_in(seeds[7], 71), 0)
    inputs = normal_values(seeds[2], (SEQS, FRAMES, D), 1.0, 6.0, ((0, 4), (1, 8)))
    cotangent = normal_values(seeds[3], (SEQS, FRAMES, D), 1.0, 6.0, ((0, 4), (1, 8)))
    out_weight = normal_values(seeds[4], (HW, D), HW ** -0.5, 0.21875, ((0, 4),))
    conv_kernel = normal_values(seeds[5], (KW, D), KW ** -0.5, 1.0, ((1, 4),))
    utt_starts = draw_utt_starts(jax.random.fold_in(seeds[7], 71), 0)
    return dict(queries=queries, keys_values=keys_values, inputs=inputs, cotangent=cotangent, out_weight=out_weight, conv_kernel=conv_kernel, utt_starts=utt_starts)


masked_score = -1e+30

def segment_ids(starts_row, positions):
    return lax.optimization_barrier(jnp.sum((starts_row[None, :] <= positions[:, None]).astype(jnp.int32), axis=1)) - 1

def attend_sequence(query_rows, kv_rows, segments):
    window_half = WIN // 2
    padded_kv = jnp.pad(kv_rows, ((window_half, window_half), (0, 0)))
    padded_seg = jnp.pad(segments, (window_half, window_half), constant_values=-1)
    block_rows = min(FRAMES, 512)
    block_count = FRAMES // block_rows
    key_span = block_rows + 2 * window_half
    key_offset = jnp.arange(key_span, dtype=jnp.int32)[None, :] - jnp.arange(block_rows, dtype=jnp.int32)[:, None]
    in_window = (key_offset >= 0) & (key_offset <= 2 * window_half)

    def one_block(block_index):
        row_start = (block_index * block_rows).astype(jnp.int32)
        query_block = lax.dynamic_slice_in_dim(query_rows, row_start, block_rows, 0).astype(jnp.float32)
        query_block = query_block.reshape(block_rows, HEADS_W, HD)
        kv_block = lax.dynamic_slice_in_dim(padded_kv, row_start, key_span, 0).astype(jnp.float32)
        key_part = kv_block[:, :HW].reshape(key_span, HEADS_W, HD)
        value_part = kv_block[:, HW:].reshape(key_span, HEADS_W, HD)
        query_seg = lax.dynamic_slice_in_dim(segments, row_start, block_rows, 0)
        key_seg = lax.dynamic_slice_in_dim(padded_seg, row_start, key_span, 0)
        allowed = in_window & (query_seg[:, None] == key_seg[None, :])
        scores = jnp.einsum('qhe,khe->hqk', query_block, key_part) / math.sqrt(HD)
        scores = jnp.where(allowed[None], scores, masked_score)
        row_max = lax.optimization_barrier(jnp.max(scores, axis=2, keepdims=True))
        exp_scores = jnp.exp(scores - row_max)
        attn_probs = (exp_scores / lax.optimization_barrier(jnp.sum(exp_scores, axis=2, keepdims=True))).astype(jnp.bfloat16)
        context = jnp.einsum('hqk,khe->qhe', attn_probs.astype(jnp.float32), value_part)
        return context.reshape(block_rows, HW).astype(jnp.bfloat16)
    blocks = lax.map(one_block, jnp.arange(block_count, dtype=jnp.int32))
    return blocks.reshape(FRAMES, HW)

def conv_sequence(residual, cotangent_rows, segments, kernel_float):
    conv_lead = KW // 2
    padded_res = jnp.pad(residual.astype(jnp.float32), ((conv_lead, conv_lead), (0, 0)))
    padded_seg = jnp.pad(segments, (conv_lead, conv_lead), constant_values=-1)
    conv_out = jnp.zeros((FRAMES, D), jnp.float32)
    for offset in range(KW):
        same_utt = (padded_seg[offset:offset + FRAMES] == segments)[:, None]
        conv_out = conv_out + jnp.where(same_utt, kernel_float[offset] * padded_res[offset:offset + FRAMES], 0.0)
    gate_sig = jax.nn.sigmoid(conv_out)
    gated_grad = cotangent_rows.astype(jnp.float32) * gate_sig * (1.0 + conv_out * (1.0 - gate_sig))
    padded_grad = jnp.pad(gated_grad, ((conv_lead, conv_lead), (0, 0)))
    back_sum = cotangent_rows.astype(jnp.float32)
    kernel_rows = []
    for offset in range(KW):
        lower = KW - offset
        same_back = (padded_seg[lower:lower + FRAMES] == segments)[:, None]
        back_sum = back_sum + jnp.where(same_back, kernel_float[offset] * padded_grad[lower:lower + FRAMES], 0.0)
        same_utt = (padded_seg[offset:offset + FRAMES] == segments)[:, None]
        kernel_rows.append(lax.optimization_barrier(jnp.sum(jnp.where(same_utt, gated_grad * padded_res[offset:offset + FRAMES], 0.0), axis=0)))
    return (back_sum.astype(jnp.bfloat16), jnp.stack(kernel_rows))

def reference(queries, keys_values, inputs, cotangent, out_weight, conv_kernel, utt_starts):
    kernel_float = conv_kernel.astype(jnp.float32)

    def one_sequence(sequence_item):
        query_rows, kv_rows, input_rows, cotangent_rows, starts_row = sequence_item
        segments = segment_ids(starts_row, jnp.arange(FRAMES, dtype=jnp.int32))
        context = attend_sequence(query_rows, kv_rows, segments)
        residual = (input_rows.astype(jnp.float32) + jnp.dot(context, out_weight, preferred_element_type=jnp.float32)).astype(jnp.bfloat16)
        residual_grad, kernel_rows = conv_sequence(residual, cotangent_rows, segments, kernel_float)
        context_grad = lax.dot_general(residual_grad, out_weight, (((1,), (1,)), ((), ())), preferred_element_type=jnp.float32).astype(jnp.bfloat16)
        weight_rows = lax.dot_general(context, residual_grad, (((0,), (0,)), ((), ())), preferred_element_type=jnp.float32)
        return (context_grad, weight_rows, kernel_rows)
    context_grad, weight_parts, kernel_parts = lax.map(one_sequence, (queries, keys_values, inputs, cotangent, utt_starts))
    grad_scale = 1.0 / math.sqrt(SEQS * FRAMES)
    return (context_grad, lax.optimization_barrier(jnp.sum(weight_parts, axis=0)) * grad_scale, lax.optimization_barrier(jnp.sum(kernel_parts, axis=0)) * grad_scale)
```

```python
import functools
import math

import jax
import jax.numpy as jnp
from jax import lax
from jax.experimental import pallas as pl
from jax.experimental.pallas import tpu as pltpu
from jax.sharding import PartitionSpec as P

HEADS_W = 8
KW = 32
WIN = 128


masked_score = -1e30


def with_halo(x, sides, width):
    for axis, dim in sides:
        devices, length = (lax.axis_size(axis), x.shape[dim])
        up = [(i, (i + 1) % devices) for i in range(devices - 1)]
        down = [(j, i) for i, j in up]
        last = lax.slice_in_dim(x, length - width, length, axis=dim)
        initial = lax.slice_in_dim(x, 0, width, axis=dim)
        before = lax.ppermute(last, axis, up)
        after = lax.ppermute(initial, axis, down)
        x = jnp.concatenate([before, x, after], axis=dim)
    return x


def segment_ids(starts_row, positions):
    return jnp.sum((starts_row[None, :] <= positions[:, None]).astype(jnp.int32), axis=1) - 1


def shards(queries, keys_values, inputs, cotangent, out_weight, conv_kernel, utt_starts):
    query_rows = queries[0]
    kv_rows = keys_values[0]
    input_rows = inputs[0]
    cotangent_rows = cotangent[0]
    starts_row = utt_starts[0]
    local_frames = query_rows.shape[0]
    head_width = query_rows.shape[1]
    head_size = head_width // HEADS_W
    window_half = WIN // 2
    conv_reach = KW - 1
    conv_lead = KW // 2
    conv_span = local_frames + KW - 1
    frames_total = local_frames * lax.axis_size("tm")
    first_frame = lax.axis_index("tm") * local_frames
    full_weight, full_kernel = (
        lax.all_gather(out_weight, "fsdp", axis=0, tiled=True),
        lax.all_gather(conv_kernel, "fsdp", axis=1, tiled=True),
    )
    kv_ext = with_halo(kv_rows, (("tm", 0),), window_half)
    key_span = local_frames + 2 * window_half
    key_positions = first_frame - window_half + jnp.arange(key_span, dtype=jnp.int32)
    key_seg = jnp.where(key_positions < frames_total, segment_ids(starts_row, key_positions), -1)
    query_seg = segment_ids(starts_row, first_frame + jnp.arange(local_frames, dtype=jnp.int32))
    key_offset = (
        jnp.arange(key_span, dtype=jnp.int32)[None, :]
        - jnp.arange(local_frames, dtype=jnp.int32)[:, None]
    )
    allowed = (
        (key_offset >= 0)
        & (key_offset <= 2 * window_half)
        & (query_seg[:, None] == key_seg[None, :])
    )
    query_heads = query_rows.reshape(local_frames, HEADS_W, head_size)
    key_heads = kv_ext[:, :head_width].reshape(key_span, HEADS_W, head_size)
    value_heads = kv_ext[:, head_width:].reshape(key_span, HEADS_W, head_size)
    scores = jnp.einsum(
        "qhe,khe->hqk", query_heads, key_heads, preferred_element_type=jnp.float32
    ) / math.sqrt(head_size)
    scores = jnp.where(allowed[None], scores, masked_score)
    row_max = jnp.max(scores, axis=2, keepdims=True)
    exp_scores = jnp.exp(scores - row_max)
    attn_probs = (exp_scores / jnp.sum(exp_scores, axis=2, keepdims=True)).astype(jnp.bfloat16)
    context = jnp.einsum(
        "hqk,khe->qhe", attn_probs, value_heads, preferred_element_type=jnp.float32
    )
    context = context.reshape(local_frames, head_width).astype(jnp.bfloat16)
    residual = (
        input_rows.astype(jnp.float32)
        + jnp.dot(context, full_weight, preferred_element_type=jnp.float32)
    ).astype(jnp.bfloat16)
    stacked_rims = with_halo(jnp.stack([residual, cotangent_rows]), (("tm", 1),), conv_reach)
    residual_ext = stacked_rims[0]
    cotangent_ext = stacked_rims[1][conv_lead : conv_lead + conv_span]
    residual_positions = (
        first_frame - conv_reach + jnp.arange(local_frames + 2 * conv_reach, dtype=jnp.int32)
    )
    residual_seg = segment_ids(starts_row, residual_positions)
    conv_seg = residual_seg[conv_lead : conv_lead + conv_span]
    own_seg = residual_seg[conv_reach : conv_reach + local_frames]
    kernel_float = full_kernel.astype(jnp.float32)
    conv_out = jnp.zeros((conv_span, residual.shape[1]), jnp.float32)
    for offset in range(KW):
        same_utt = (conv_seg == residual_seg[offset : offset + conv_span])[:, None]
        conv_out = conv_out + jnp.where(
            same_utt,
            kernel_float[offset] * residual_ext[offset : offset + conv_span].astype(jnp.float32),
            0.0,
        )
    gate_sig = jax.nn.sigmoid(conv_out)
    gated_grad = cotangent_ext.astype(jnp.float32) * gate_sig * (1.0 + conv_out * (1.0 - gate_sig))
    back_sum = cotangent_rows.astype(jnp.float32)
    own_lower = conv_lead - 1
    own_grad = gated_grad[own_lower : own_lower + local_frames]
    own_conv_seg = conv_seg[own_lower : own_lower + local_frames]
    for offset in range(KW):
        lower = KW - 1 - offset
        same_back = (conv_seg[lower : lower + local_frames] == own_seg)[:, None]
        back_sum = back_sum + jnp.where(
            same_back, kernel_float[offset] * gated_grad[lower : lower + local_frames], 0.0
        )
    products = jnp.stack(
        [
            jnp.where(
                (
                    own_conv_seg
                    == residual_seg[own_lower + offset : own_lower + offset + local_frames]
                )[:, None],
                own_grad
                * residual_ext[own_lower + offset : own_lower + offset + local_frames].astype(
                    jnp.float32
                ),
                0.0,
            )
            for offset in range(KW)
        ]
    )
    kernel_part = jnp.sum(products, axis=1)
    residual_grad = back_sum.astype(jnp.bfloat16)
    context_grad = lax.dot_general(
        residual_grad, full_weight, (((1,), (1,)), ((), ())), preferred_element_type=jnp.float32
    ).astype(jnp.bfloat16)
    grad_scale = 1.0 / math.sqrt(lax.axis_size("fsdp") * queries.shape[0] * frames_total)
    weight_part = (
        lax.dot_general(
            context, residual_grad, (((0,), (0,)), ((), ())), preferred_element_type=jnp.float32
        )
        * grad_scale
    )
    weight_share, kernel_share = (
        lax.psum_scatter(
            weight_part.astype(jnp.bfloat16), "fsdp", scatter_dimension=0, tiled=True
        ).astype(jnp.float32),
        lax.psum_scatter(
            (kernel_part * grad_scale).astype(jnp.bfloat16), "fsdp", scatter_dimension=1, tiled=True
        ).astype(jnp.float32),
    )
    weight_grad, kernel_grad = lax.psum((weight_share, kernel_share), "tm")
    return (context_grad[None], weight_grad, kernel_grad)


MESH = pl.DeviceIdType.MESH
KEY_PAD = 96
ROW_PAD = 32
COT_PAD = 16
BLOCK = 64
LANES = 128


def dot(a, b):
    return jnp.dot(a, b, preferred_element_type=jnp.float32)


def dot_t(a, b):
    return lax.dot_general(a, b, (((1,), (1,)), ((), ())), preferred_element_type=jnp.float32)


def block_kernel(
    nt, nf,
    starts_ref, q_ref, kv_ref, in_ref, cot_ref, w_ref, ck_ref,
    cg_ref, wg_ref, kg_ref,
    kvx, qx, inx, cotx, wfull, kall, kf, seg, m1, ctx, ctx_t, res, gs, rg, kgs,
    part, own, asrc, abuf, bsrc, bbuf, fsum, csrc, cbuf, gbuf,
    kgsrc, kgb, kgcs, kgc, kgds, kgd,
    hs, hr, ws, wr, fs, fr, ks, kr, as_, ar, bs, br, cs, cr, gsn, grc, ds_, dr,
    kbs, kbr, kcs, kcr, kds, kdr,
):
    nz = nt // 2
    t = lax.axis_index("tm")
    f = lax.axis_index("fsdp")
    z = lax.div(t, 2)
    c = lax.rem(t, 2)
    sib = t + 1 - 2 * c
    rows = q_ref.shape[0]
    shard = w_ref.shape[0]
    half = shard // 2
    width = in_ref.shape[1]
    head_width = q_ref.shape[1]
    head_size = head_width // HEADS_W
    chunks = width // LANES
    per_shard = chunks // nf
    chunk_w = width // nz
    per_piece = chunks // nz
    ext = rows + 2 * ROW_PAD
    span = rows + 2 * COT_PAD
    first = t * rows
    total = nt * rows

    def other_f(i):
        return lax.rem(f + i, nf)

    def from_f(i):
        return lax.rem(f + nf - i, nf)

    def other_z(i):
        return lax.rem(z + i, nz)

    def copy(src, dst, send, recv, tm, fsdp):
        return pltpu.make_async_remote_copy(
            src_ref=src, dst_ref=dst, send_sem=send, recv_sem=recv,
            device_id={"tm": tm, "fsdp": fsdp}, device_id_type=MESH,
        )

    barrier = pltpu.get_barrier_semaphore()

    def greet(tm, fsdp):
        pl.semaphore_signal(
            barrier, inc=1, device_id={"tm": tm, "fsdp": fsdp}, device_id_type=MESH
        )

    for i in range(1, nf):
        greet(t, other_f(i))
    for i in range(1, nz):
        greet(2 * other_z(i) + c, f)

    @pl.when(t > 0)
    def _():
        greet(t - 1, f)

    @pl.when(t < nt - 1)
    def _():
        greet(t + 1, f)

    near = jnp.minimum(t, 1) + jnp.minimum(nt - 1 - t, 1)
    pl.semaphore_wait(barrier, nf - 1 + nz - 1 + near)

    halo = ((kv_ref, kvx, KEY_PAD), (q_ref, qx, ROW_PAD), (in_ref, inx, ROW_PAD), (cot_ref, cotx, COT_PAD))

    def up_copy(n):
        src, dst, pad = halo[n]
        return copy(
            src.at[pl.ds(rows - pad, pad)], dst.at[pl.ds(0, pad)], hs.at[0, n], hr.at[0, n], t + 1, f
        )

    def down_copy(n):
        src, dst, pad = halo[n]
        return copy(
            src.at[pl.ds(0, pad)], dst.at[pl.ds(pad + rows, pad)], hs.at[1, n], hr.at[1, n], t - 1, f
        )

    @pl.when(t < nt - 1)
    def _():
        for n in range(4):
            up_copy(n).start()

    @pl.when(t > 0)
    def _():
        for n in range(4):
            down_copy(n).start()

    def rows_of(owner, core):
        return pl.ds(pl.multiple_of(owner * shard + core * half, 16), half)

    w_copies = [
        copy(
            w_ref.at[pl.ds(pl.multiple_of(c * half, 16), half)], wfull.at[rows_of(f, c)],
            ws.at[i], wr.at[i], t, other_f(i),
        )
        for i in range(1, nf)
    ]
    k_copies = [
        copy(ck_ref, kall.at[f], ks.at[i], kr.at[i], t, other_f(i)) for i in range(1, nf)
    ]
    for w_copy in w_copies:
        w_copy.start()
    for k_copy in k_copies:
        k_copy.start()

    @pl.when(t == 0)
    def _():
        for src, dst, pad in halo:
            dst[0:pad] = jnp.zeros((pad, dst.shape[1]), dst.dtype)

    @pl.when(t == nt - 1)
    def _():
        for src, dst, pad in halo:
            dst[pad + rows : 2 * pad + rows] = jnp.zeros((pad, dst.shape[1]), dst.dtype)

    for src, dst, pad in halo:
        dst[pad : pad + rows] = src[...]
    wfull[pl.ds(pl.multiple_of(f * shard, 16), shard)] = w_ref[...]
    kall[f] = ck_ref[...]

    utts = starts_ref.shape[1]

    def segments(positions):
        found = jnp.full(positions.shape, -1.0, jnp.float32)
        for u in range(utts):
            found = found + jnp.where(starts_ref[0, u] <= positions, 1.0, 0.0)
        return jnp.where(positions < total, found, -1.0)

    seg[...] = segments(lax.broadcasted_iota(jnp.int32, (ext, LANES), 0) + (first - ROW_PAD))

    for k in range(KW + 1):
        m1[k] = jnp.where(seg[k : k + span] == seg[COT_PAD : COT_PAD + span], 1.0, 0.0)

    @pl.when(t > 0)
    def _():
        for n in range(4):
            up_copy(n).wait_recv()

    @pl.when(t < nt - 1)
    def _():
        for n in range(4):
            down_copy(n).wait_recv()

    keys = 2 * LANES
    key_rows = rows + 2 * KEY_PAD
    scale = 1.0 / math.sqrt(head_size)
    lane = lax.broadcasted_iota(jnp.int32, (1, keys), 1)
    for b in range(ext // BLOCK):
        start = min(BLOCK * b, key_rows - keys)
        key_seg = segments(lane + (first - KEY_PAD + start))
        query_seg = seg[BLOCK * b : BLOCK * (b + 1)]
        query_seg = jnp.concatenate([query_seg, query_seg], axis=1)
        gap = (
            lax.broadcasted_iota(jnp.int32, (BLOCK, keys), 1)
            - lax.broadcasted_iota(jnp.int32, (BLOCK, keys), 0)
            + (start - KEY_PAD - BLOCK * b + ROW_PAD)
        )
        allowed = (gap >= -(WIN // 2)) & (gap <= WIN // 2) & (query_seg == key_seg)
        bias = jnp.where(allowed, 0.0, masked_score)
        bias = jnp.concatenate([bias, bias], axis=0)
        for g in range(HEADS_W // 4):
            pairs = []
            for p in range(2):
                base = 4 * head_size * g + LANES * p
                lower = (2 * head_size - LANES) * p
                middle, upper = lower + head_size, lower + 2 * head_size
                in_a = jnp.where((lane >= lower) & (lane < middle), 1.0, 0.0)
                in_b = jnp.where((lane >= middle) & (lane < upper), 1.0, 0.0)
                query = qx[BLOCK * b : BLOCK * (b + 1), base : base + keys]
                query = jnp.concatenate(
                    [query * in_a.astype(jnp.bfloat16), query * in_b.astype(jnp.bfloat16)], axis=0
                )
                scores = dot_t(query, kvx[start : start + keys, base : base + keys]) * scale + bias
                weights = jnp.exp(scores - jnp.max(scores, axis=1, keepdims=True))
                probs = (weights / jnp.sum(weights, axis=1, keepdims=True)).astype(jnp.bfloat16)
                value = dot(
                    probs,
                    kvx[start : start + keys, head_width + base : head_width + base + keys],
                )
                pairs.append(value[:BLOCK] * in_a + value[BLOCK:] * in_b)
            joined = jnp.concatenate(
                [
                    pairs[0][:, :LANES],
                    pairs[0][:, LANES:] + pairs[1][:, :LANES],
                    pairs[1][:, LANES:],
                ],
                axis=1,
            )
            ctx[BLOCK * b : BLOCK * (b + 1), 4 * head_size * g : 4 * head_size * (g + 1)] = (
                joined.astype(jnp.bfloat16)
            )
    ctx_t[...] = ctx[ROW_PAD : ROW_PAD + rows].astype(jnp.float32).T.astype(jnp.bfloat16)

    def forward(i):
        piece = wfull.at[rows_of(from_f(i), c)]
        return copy(piece, piece, fs.at[i], fr.at[i], sib, f)

    for i in range(1, nf):
        w_copies[i - 1].wait_recv()
        forward(i).start()
    for i in range(1, nf):
        k_copies[i - 1].wait_recv()
    for s in range(nf):
        for i in range(per_shard):
            kf[s * per_shard + i] = kall[s, :, LANES * i : LANES * (i + 1)].astype(jnp.float32)
    for i in range(1, nf):
        forward(i).wait_recv()

    for j in range(nz):
        columns = slice(chunk_w * j, chunk_w * (j + 1))
        out = inx[:, columns].astype(jnp.float32) + dot(ctx[...], wfull[:, columns])
        out = out.astype(jnp.bfloat16).astype(jnp.float32)
        for i in range(per_piece):
            res[per_piece * j + i] = out[:, LANES * i : LANES * (i + 1)]

    def conv_chunk(n, carry):
        columns = pl.ds(pl.multiple_of(n * LANES, LANES), LANES)
        conv = jnp.zeros((span, LANES), jnp.float32)
        for b in range(8):
            shifted = res[n, pl.ds(b, span + 24), :]
            for a in range(KW // 8):
                k = 8 * a + b
                conv = conv + m1[k] * (kf[n, k : k + 1, :] * shifted[8 * a : 8 * a + span])
        sig = jax.nn.sigmoid(conv)
        cot = cotx[:, columns].astype(jnp.float32)
        gs[...] = cot * sig * (1.0 + conv * (1.0 - sig))
        back = cot_ref[:, columns].astype(jnp.float32)
        mid = slice(COT_PAD, COT_PAD + rows)
        for b in range(8):
            low = 8 if b == 0 else 0
            shifted = gs[b + low : b + low + rows + 24]
            for a in range(KW // 8):
                o = 8 * a + b + low
                k = KW - o
                back = back + m1[o, mid] * (kf[n, k : k + 1, :] * shifted[8 * a : 8 * a + rows])
        rg[:, columns] = back.astype(jnp.bfloat16)
        grad = gs[mid]
        for b in range(8):
            shifted = res[n, pl.ds(COT_PAD + b, rows + 24), :]
            for a in range(KW // 8):
                k = 8 * a + b
                prod = m1[k, mid] * grad * shifted[8 * a : 8 * a + rows]
                prod = jnp.sum(prod.reshape(rows // 8, 8, LANES), axis=0)
                kgs[n, k : k + 1, :] = jnp.sum(prod, axis=0, keepdims=True)
        return carry

    def a_copy(j):
        return copy(asrc.at[j], abuf.at[j], as_.at[j], ar.at[j], sib, f)

    def b_copy(j, i):
        return copy(
            bsrc.at[j, other_f(i)], bbuf.at[j, i], bs.at[j, i], br.at[j, i], t, other_f(i)
        )

    def c_copy(j):
        return copy(csrc.at[j], cbuf.at[z], cs.at[j], cr.at[z], 2 * j + c, f)

    def finish_a(j):
        a_copy(j).wait_recv()
        for s in range(nf):
            bsrc[j, s] = (own[j, s] + abuf[j, s].astype(jnp.float32)).astype(jnp.bfloat16)
        for i in range(1, nf):
            b_copy(j, i).start()

    def finish_b(j):
        acc = own[j, f] + abuf[j, f].astype(jnp.float32)
        for i in range(1, nf):
            b_copy(j, i).wait_recv()
            acc = acc + bbuf[j, i].astype(jnp.float32)

        @pl.when(z == j)
        def _():
            fsum[...] = acc

        @pl.when(z != j)
        def _():
            csrc[j] = acc.astype(jnp.bfloat16)
            c_copy(j).start()

    for j in range(nz):
        lax.fori_loop(per_piece * j, per_piece * (j + 1), conv_chunk, 0)
        part[...] = dot(ctx_t[...], rg[:, chunk_w * j : chunk_w * (j + 1)])
        for s in range(nf):
            own[j, s] = part[rows_of(s, c)]
            asrc[j, s] = part[rows_of(s, 1 - c)].astype(jnp.bfloat16)
        a_copy(j).start()
        if j >= 1:
            finish_a(j - 1)
        if j >= 2:
            finish_b(j - 2)

    def kb_copy(i):
        return copy(kgsrc.at[other_f(i)], kgb.at[i], kbs.at[i], kbr.at[i], t, other_f(i))

    for s in range(nf):
        for i in range(per_shard):
            kgsrc[s, i] = kgs[s * per_shard + i].astype(jnp.bfloat16)
    for i in range(1, nf):
        kb_copy(i).start()
    finish_a(nz - 1)
    if nz >= 2:
        finish_b(nz - 2)
    cg_ref[...] = dot_t(rg[...], wfull[...]).astype(jnp.bfloat16)

    kg_sum = kgs[pl.ds(f * per_shard, per_shard)]
    for i in range(1, nf):
        kb_copy(i).wait_recv()
        kg_sum = kg_sum + kgb[i].astype(jnp.float32)
    kgcs[...] = kg_sum.astype(jnp.bfloat16)

    def kc_copy(i):
        return copy(kgcs, kgc.at[z], kcs.at[i], kcr.at[z], 2 * other_z(i) + c, f)

    def kc_from(i):
        s = other_z(i)
        return copy(kgcs, kgc.at[s], kcs.at[i], kcr.at[s], 2 * s + c, f)

    for i in range(1, nz):
        kc_copy(i).start()
    kgc[z] = kgcs[...]
    finish_b(nz - 1)

    def c_from(i):
        s = other_z(i)
        return copy(csrc.at[0], cbuf.at[s], cs.at[0], cr.at[s], 2 * s + c, f)

    final = fsum[...]
    for i in range(1, nz):
        c_from(i).wait_recv()
        final = final + cbuf[other_z(i)].astype(jnp.float32)
    gbuf[c, z] = final.astype(jnp.bfloat16)

    def g_copy(i):
        piece = gbuf.at[c, z]
        return copy(piece, piece, gsn.at[i], grc.at[z], 2 * other_z(i) + c, f)

    def g_from(i):
        s = other_z(i)
        piece = gbuf.at[c, s]
        return copy(piece, piece, gsn.at[i], grc.at[s], 2 * s + c, f)

    def d_copy(s):
        piece = gbuf.at[c, s]
        return copy(piece, piece, ds_.at[s], dr.at[s], sib, f)

    def d_from(s):
        piece = gbuf.at[1 - c, s]
        return copy(piece, piece, ds_.at[s], dr.at[s], sib, f)

    for i in range(1, nz):
        g_copy(i).start()
    d_copy(z).start()

    for i in range(1, nz):
        kc_from(i).wait_recv()
    kg_z = kgc[0].astype(jnp.float32)
    for s in range(1, nz):
        kg_z = kg_z + kgc[s].astype(jnp.float32)
    kgds[...] = kg_z.astype(jnp.bfloat16)
    kd_copy = copy(kgds, kgd, kds, kdr, sib, f)
    kd_copy.start()

    for i in range(1, nz):
        g_from(i).wait_recv()
        d_copy(other_z(i)).start()
    kd_copy.wait_recv()
    kg_all = kgds[...].astype(jnp.float32) + kgd[...].astype(jnp.float32)
    for i in range(per_shard):
        kg_ref[:, LANES * i : LANES * (i + 1)] = kg_all[i]
    mine = pl.ds(pl.multiple_of(c * half, 16), half)
    theirs = pl.ds(pl.multiple_of((1 - c) * half, 16), half)
    for s in range(nz):
        wg_ref[mine, chunk_w * s : chunk_w * (s + 1)] = gbuf[c, s]
    for i in range(nz):
        d_from(other_z(i)).wait_recv()
    for s in range(nz):
        wg_ref[theirs, chunk_w * s : chunk_w * (s + 1)] = gbuf[1 - c, s]

    @pl.when(t < nt - 1)
    def _():
        for n in range(4):
            up_copy(n).wait_send()

    @pl.when(t > 0)
    def _():
        for n in range(4):
            down_copy(n).wait_send()

    for i in range(1, nf):
        w_copies[i - 1].wait_send()
        k_copies[i - 1].wait_send()
        forward(i).wait_send()
        kb_copy(i).wait_send()
    for j in range(nz):
        a_copy(j).wait_send()
        for i in range(1, nf):
            b_copy(j, i).wait_send()

        @pl.when(z != j)
        def _():
            c_copy(j).wait_send()

    for i in range(1, nz):
        kc_copy(i).wait_send()
        g_copy(i).wait_send()
    for i in range(nz):
        d_copy(other_z(i)).wait_send()
    kd_copy.wait_send()


def fused(nt, nf, queries, keys_values, inputs, cotangent, out_weight, conv_kernel, utt_starts):
    rows, head_width = queries.shape[1:]
    width = inputs.shape[2]
    nz = nt // 2
    shard = out_weight.shape[0]
    half = shard // 2
    chunks = width // LANES
    per_shard = chunks // nf
    chunk_w = width // nz
    ext = rows + 2 * ROW_PAD
    span = rows + 2 * COT_PAD
    bf16, f32 = jnp.bfloat16, jnp.float32
    dma = pltpu.SemaphoreType.DMA
    vmem = pl.BlockSpec(memory_space=pltpu.VMEM)
    scratch = [
        ((rows + 2 * KEY_PAD, 2 * head_width), bf16),
        ((ext, head_width), bf16),
        ((ext, width), bf16),
        ((span, width), bf16),
        ((head_width, width), bf16),
        ((nf, KW, width // nf), bf16),
        ((chunks, KW, LANES), f32),
        ((ext, LANES), f32),
        ((KW + 1, span, LANES), f32),
        ((ext, head_width), bf16),
        ((head_width, rows), bf16),
        ((chunks, ext, LANES), f32),
        ((span, LANES), f32),
        ((rows, width), bf16),
        ((chunks, KW, LANES), f32),
        ((head_width, chunk_w), f32),
        ((nz, nf, half, chunk_w), f32),
        ((nz, nf, half, chunk_w), bf16),
        ((nz, nf, half, chunk_w), bf16),
        ((nz, nf, half, chunk_w), bf16),
        ((nz, nf, half, chunk_w), bf16),
        ((half, chunk_w), f32),
        ((nz, half, chunk_w), bf16),
        ((nz, half, chunk_w), bf16),
        ((2, nz, half, chunk_w), bf16),
        ((nf, per_shard, KW, LANES), bf16),
        ((nf, per_shard, KW, LANES), bf16),
        ((per_shard, KW, LANES), bf16),
        ((nz, per_shard, KW, LANES), bf16),
        ((per_shard, KW, LANES), bf16),
        ((per_shard, KW, LANES), bf16),
    ]
    sems = [
        (2, 4), (2, 4), (nf,), (nf,), (nf,), (nf,), (nf,), (nf,), (nz,), (nz,), (nz, nf), (nz, nf),
        (nz,), (nz,), (nz,), (nz,), (nz,), (nz,), (nf,), (nf,), (nz,), (nz,),
    ]
    context_grad, weight_grad, kernel_grad = pl.pallas_call(
        functools.partial(block_kernel, nt, nf),
        out_shape=(
            jax.ShapeDtypeStruct((rows, head_width), bf16),
            jax.ShapeDtypeStruct((shard, width), bf16),
            jax.ShapeDtypeStruct((KW, width // nf), f32),
        ),
        in_specs=[pl.BlockSpec(memory_space=pltpu.SMEM)] + [vmem] * 6,
        out_specs=(vmem, vmem, vmem),
        scratch_shapes=[pltpu.VMEM(*s) for s in scratch]
        + [dma(s) for s in sems]
        + [dma, dma],
        compiler_params=pltpu.CompilerParams(
            collective_id=0, has_side_effects=True, vmem_limit_bytes=48 * 1024 * 1024
        ),
    )(utt_starts, queries[0], keys_values[0], inputs[0], cotangent[0], out_weight, conv_kernel)
    grad_scale = 1.0 / math.sqrt(nf * queries.shape[0] * nt * rows)
    return (
        context_grad[None],
        weight_grad.astype(jnp.float32) * grad_scale,
        kernel_grad * grad_scale,
    )


def fits(nt, nf, queries, keys_values, inputs, cotangent, out_weight, conv_kernel, utt_starts):
    rows, head_width = queries.shape[1:]
    width = inputs.shape[2]
    return (
        queries.shape[0] == 1
        and rows == 2 * BLOCK
        and nt % 2 == 0
        and nt >= 4
        and (width // LANES) % (nt // 2) == 0
        and (width // LANES) % nf == 0
        and out_weight.shape[0] % 32 == 0
        and head_width * LANES == HEADS_W * 96 * LANES
    )


def solution(mesh):
    nt, nf = mesh.shape["tm"], mesh.shape["fsdp"]

    def body(*arrays):
        if fits(nt, nf, *arrays):
            return fused(nt, nf, *arrays)
        return shards(*arrays)

    return jax.shard_map(
        body,
        mesh=mesh,
        in_specs=(
            P("fsdp", "tm", None),
            P("fsdp", "tm", None),
            P("fsdp", "tm", None),
            P("fsdp", "tm", None),
            P("fsdp", None),
            P(None, "fsdp"),
            P("fsdp", None),
        ),
        out_specs=(P("fsdp", "tm", None), P("fsdp", None), P(None, "fsdp")),
        check_vma=False,
    )
```

```python
import functools
import math

import jax
import jax.numpy as jnp
from jax import lax
from jax.experimental import pallas as pl
from jax.experimental.pallas import tpu as pltpu
from jax.sharding import PartitionSpec as P

HEADS_W = 8
KW = 32
WIN = 128


masked_score = -1e30


def with_halo(x, sides, width):
    for axis, dim in sides:
        devices, length = (lax.axis_size(axis), x.shape[dim])
        up = [(i, (i + 1) % devices) for i in range(devices - 1)]
        down = [(j, i) for i, j in up]
        last = lax.slice_in_dim(x, length - width, length, axis=dim)
        initial = lax.slice_in_dim(x, 0, width, axis=dim)
        before = lax.ppermute(last, axis, up)
        after = lax.ppermute(initial, axis, down)
        x = jnp.concatenate([before, x, after], axis=dim)
    return x


def segment_ids(starts_row, positions):
    return jnp.sum((starts_row[None, :] <= positions[:, None]).astype(jnp.int32), axis=1) - 1


def shards(queries, keys_values, inputs, cotangent, out_weight, conv_kernel, utt_starts):
    query_rows = queries[0]
    kv_rows = keys_values[0]
    input_rows = inputs[0]
    cotangent_rows = cotangent[0]
    starts_row = utt_starts[0]
    local_frames = query_rows.shape[0]
    head_width = query_rows.shape[1]
    head_size = head_width // HEADS_W
    window_half = WIN // 2
    conv_reach = KW - 1
    conv_lead = KW // 2
    conv_span = local_frames + KW - 1
    frames_total = local_frames * lax.axis_size("tm")
    first_frame = lax.axis_index("tm") * local_frames
    full_weight, full_kernel = (
        lax.all_gather(out_weight, "fsdp", axis=0, tiled=True),
        lax.all_gather(conv_kernel, "fsdp", axis=1, tiled=True),
    )
    kv_ext = with_halo(kv_rows, (("tm", 0),), window_half)
    key_span = local_frames + 2 * window_half
    key_positions = first_frame - window_half + jnp.arange(key_span, dtype=jnp.int32)
    key_seg = jnp.where(key_positions < frames_total, segment_ids(starts_row, key_positions), -1)
    query_seg = segment_ids(starts_row, first_frame + jnp.arange(local_frames, dtype=jnp.int32))
    key_offset = (
        jnp.arange(key_span, dtype=jnp.int32)[None, :]
        - jnp.arange(local_frames, dtype=jnp.int32)[:, None]
    )
    allowed = (
        (key_offset >= 0)
        & (key_offset <= 2 * window_half)
        & (query_seg[:, None] == key_seg[None, :])
    )
    query_heads = query_rows.reshape(local_frames, HEADS_W, head_size)
    key_heads = kv_ext[:, :head_width].reshape(key_span, HEADS_W, head_size)
    value_heads = kv_ext[:, head_width:].reshape(key_span, HEADS_W, head_size)
    scores = jnp.einsum(
        "qhe,khe->hqk", query_heads, key_heads, preferred_element_type=jnp.float32
    ) / math.sqrt(head_size)
    scores = jnp.where(allowed[None], scores, masked_score)
    row_max = jnp.max(scores, axis=2, keepdims=True)
    exp_scores = jnp.exp(scores - row_max)
    attn_probs = (exp_scores / jnp.sum(exp_scores, axis=2, keepdims=True)).astype(jnp.bfloat16)
    context = jnp.einsum(
        "hqk,khe->qhe", attn_probs, value_heads, preferred_element_type=jnp.float32
    )
    context = context.reshape(local_frames, head_width).astype(jnp.bfloat16)
    residual = (
        input_rows.astype(jnp.float32)
        + jnp.dot(context, full_weight, preferred_element_type=jnp.float32)
    ).astype(jnp.bfloat16)
    stacked_rims = with_halo(jnp.stack([residual, cotangent_rows]), (("tm", 1),), conv_reach)
    residual_ext = stacked_rims[0]
    cotangent_ext = stacked_rims[1][conv_lead : conv_lead + conv_span]
    residual_positions = (
        first_frame - conv_reach + jnp.arange(local_frames + 2 * conv_reach, dtype=jnp.int32)
    )
    residual_seg = segment_ids(starts_row, residual_positions)
    conv_seg = residual_seg[conv_lead : conv_lead + conv_span]
    own_seg = residual_seg[conv_reach : conv_reach + local_frames]
    kernel_float = full_kernel.astype(jnp.float32)
    conv_out = jnp.zeros((conv_span, residual.shape[1]), jnp.float32)
    for offset in range(KW):
        same_utt = (conv_seg == residual_seg[offset : offset + conv_span])[:, None]
        conv_out = conv_out + jnp.where(
            same_utt,
            kernel_float[offset] * residual_ext[offset : offset + conv_span].astype(jnp.float32),
            0.0,
        )
    gate_sig = jax.nn.sigmoid(conv_out)
    gated_grad = cotangent_ext.astype(jnp.float32) * gate_sig * (1.0 + conv_out * (1.0 - gate_sig))
    back_sum = cotangent_rows.astype(jnp.float32)
    own_lower = conv_lead - 1
    own_grad = gated_grad[own_lower : own_lower + local_frames]
    own_conv_seg = conv_seg[own_lower : own_lower + local_frames]
    for offset in range(KW):
        lower = KW - 1 - offset
        same_back = (conv_seg[lower : lower + local_frames] == own_seg)[:, None]
        back_sum = back_sum + jnp.where(
            same_back, kernel_float[offset] * gated_grad[lower : lower + local_frames], 0.0
        )
    products = jnp.stack(
        [
            jnp.where(
                (
                    own_conv_seg
                    == residual_seg[own_lower + offset : own_lower + offset + local_frames]
                )[:, None],
                own_grad
                * residual_ext[own_lower + offset : own_lower + offset + local_frames].astype(
                    jnp.float32
                ),
                0.0,
            )
            for offset in range(KW)
        ]
    )
    kernel_part = jnp.sum(products, axis=1)
    residual_grad = back_sum.astype(jnp.bfloat16)
    context_grad = lax.dot_general(
        residual_grad, full_weight, (((1,), (1,)), ((), ())), preferred_element_type=jnp.float32
    ).astype(jnp.bfloat16)
    grad_scale = 1.0 / math.sqrt(lax.axis_size("fsdp") * queries.shape[0] * frames_total)
    weight_part = (
        lax.dot_general(
            context, residual_grad, (((0,), (0,)), ((), ())), preferred_element_type=jnp.float32
        )
        * grad_scale
    )
    weight_share, kernel_share = (
        lax.psum_scatter(
            weight_part.astype(jnp.bfloat16), "fsdp", scatter_dimension=0, tiled=True
        ).astype(jnp.float32),
        lax.psum_scatter(
            (kernel_part * grad_scale).astype(jnp.bfloat16), "fsdp", scatter_dimension=1, tiled=True
        ).astype(jnp.float32),
    )
    weight_grad, kernel_grad = lax.psum((weight_share, kernel_share), "tm")
    return (context_grad[None], weight_grad, kernel_grad)


MESH = pl.DeviceIdType.MESH
KEY_PAD = 96
ROW_PAD = 32
COT_PAD = 16
BLOCK = 64
LANES = 128


def dot(a, b):
    return jnp.dot(a, b, preferred_element_type=jnp.float32)


def dot_t(a, b):
    return lax.dot_general(a, b, (((1,), (1,)), ((), ())), preferred_element_type=jnp.float32)


def block_kernel(
    nt, nf,
    starts_ref, q_ref, kv_ref, in_ref, cot_ref, w_ref, ck_ref,
    cg_ref, wg_ref, kg_ref,
    kvx, qx, inx, cotx, wfull, kall, kf, seg, m1, ctx, ctx_t, res, gs, rg, kgs, kgp,
    part, own, asrc, abuf, bsrc, bbuf, fsum, csrc, cbuf, gbuf,
    kgsrc, kgb, kgcs, kgc, kgds, kgd,
    ls, hs, hr, ws, wr, fs, fr, ks, kr, as_, ar, bs, br, cs, cr, gsn, grc, ds_, dr,
    kbs, kbr, kcs, kcr, kds, kdr,
):
    nz = nt // 2
    t = lax.axis_index("tm")
    f = lax.axis_index("fsdp")
    z = lax.div(t, 2)
    c = lax.rem(t, 2)
    sib = t + 1 - 2 * c
    rows = q_ref.shape[0]
    shard = w_ref.shape[0]
    half = shard // 2
    width = in_ref.shape[1]
    head_width = q_ref.shape[1]
    head_size = head_width // HEADS_W
    chunks = width // LANES
    per_shard = chunks // nf
    chunk_w = width // nz
    per_piece = chunks // nz
    ext = rows + 2 * ROW_PAD
    span = rows + 2 * COT_PAD
    first = t * rows
    total = nt * rows

    def other_f(i):
        return lax.rem(f + i, nf)

    def from_f(i):
        return lax.rem(f + nf - i, nf)

    def other_z(i):
        return lax.rem(z + i, nz)

    def copy(src, dst, send, recv, tm, fsdp):
        return pltpu.make_async_remote_copy(
            src_ref=src, dst_ref=dst, send_sem=send, recv_sem=recv,
            device_id={"tm": tm, "fsdp": fsdp}, device_id_type=MESH,
        )

    halo = ((kv_ref, kvx, KEY_PAD), (q_ref, qx, ROW_PAD), (in_ref, inx, ROW_PAD), (cot_ref, cotx, COT_PAD))
    own_copies = [
        pltpu.make_async_copy(src, dst.at[pl.ds(pad, rows)], ls.at[n])
        for n, (src, dst, pad) in enumerate(halo)
    ]
    own_copies.append(
        pltpu.make_async_copy(
            w_ref, wfull.at[pl.ds(pl.multiple_of(f * shard, 16), shard)], ls.at[4]
        )
    )
    own_copies.append(pltpu.make_async_copy(ck_ref, kall.at[f], ls.at[5]))
    for own_copy in own_copies:
        own_copy.start()

    barrier = pltpu.get_barrier_semaphore()

    def greet(tm, fsdp):
        pl.semaphore_signal(
            barrier, inc=1, device_id={"tm": tm, "fsdp": fsdp}, device_id_type=MESH
        )

    for i in range(1, nf):
        greet(t, other_f(i))
    for i in range(1, nz):
        greet(2 * other_z(i) + c, f)

    @pl.when(t > 0)
    def _():
        greet(t - 1, f)

    @pl.when(t < nt - 1)
    def _():
        greet(t + 1, f)

    near = jnp.minimum(t, 1) + jnp.minimum(nt - 1 - t, 1)
    pl.semaphore_wait(barrier, nf - 1 + nz - 1 + near)

    def up_copy(n):
        src, dst, pad = halo[n]
        return copy(
            src.at[pl.ds(rows - pad, pad)], dst.at[pl.ds(0, pad)], hs.at[0, n], hr.at[0, n], t + 1, f
        )

    def down_copy(n):
        src, dst, pad = halo[n]
        return copy(
            src.at[pl.ds(0, pad)], dst.at[pl.ds(pad + rows, pad)], hs.at[1, n], hr.at[1, n], t - 1, f
        )

    @pl.when(t < nt - 1)
    def _():
        for n in range(4):
            up_copy(n).start()

    @pl.when(t > 0)
    def _():
        for n in range(4):
            down_copy(n).start()

    def rows_of(owner, core):
        return pl.ds(pl.multiple_of(owner * shard + core * half, 16), half)

    w_copies = [
        copy(
            w_ref.at[pl.ds(pl.multiple_of(c * half, 16), half)], wfull.at[rows_of(f, c)],
            ws.at[i], wr.at[i], t, other_f(i),
        )
        for i in range(1, nf)
    ]
    k_copies = [
        copy(ck_ref, kall.at[f], ks.at[i], kr.at[i], t, other_f(i)) for i in range(1, nf)
    ]
    for w_copy in w_copies:
        w_copy.start()
    for k_copy in k_copies:
        k_copy.start()

    @pl.when(t == 0)
    def _():
        for src, dst, pad in halo:
            dst[0:pad] = jnp.zeros((pad, dst.shape[1]), dst.dtype)

    @pl.when(t == nt - 1)
    def _():
        for src, dst, pad in halo:
            dst[pad + rows : 2 * pad + rows] = jnp.zeros((pad, dst.shape[1]), dst.dtype)


    utts = starts_ref.shape[1]

    def segments(positions):
        found = jnp.full(positions.shape, -1.0, jnp.float32)
        for u in range(utts):
            found = found + jnp.where(starts_ref[0, u] <= positions, 1.0, 0.0)
        return jnp.where(positions < total, found, -1.0)

    seg[...] = segments(lax.broadcasted_iota(jnp.int32, (ext, LANES), 0) + (first - ROW_PAD))

    for k in range(KW + 1):
        m1[k] = jnp.where(seg[k : k + span] == seg[COT_PAD : COT_PAD + span], 1.0, 0.0)

    @pl.when(t > 0)
    def _():
        for n in range(4):
            up_copy(n).wait_recv()

    @pl.when(t < nt - 1)
    def _():
        for n in range(4):
            down_copy(n).wait_recv()

    for own_copy in own_copies:
        own_copy.wait()

    keys = 2 * LANES
    key_rows = rows + 2 * KEY_PAD
    scale = 1.0 / math.sqrt(head_size)
    lane = lax.broadcasted_iota(jnp.int32, (1, keys), 1)
    for b in range(ext // BLOCK):
        start = min(BLOCK * b, key_rows - keys)
        key_seg = segments(lane + (first - KEY_PAD + start))
        query_seg = seg[BLOCK * b : BLOCK * (b + 1)]
        query_seg = jnp.concatenate([query_seg, query_seg], axis=1)
        gap = (
            lax.broadcasted_iota(jnp.int32, (BLOCK, keys), 1)
            - lax.broadcasted_iota(jnp.int32, (BLOCK, keys), 0)
            + (start - KEY_PAD - BLOCK * b + ROW_PAD)
        )
        allowed = (gap >= -(WIN // 2)) & (gap <= WIN // 2) & (query_seg == key_seg)
        bias = jnp.where(allowed, 0.0, masked_score)
        bias = jnp.concatenate([bias, bias], axis=0)
        for g in range(HEADS_W // 4):
            pairs = []
            for p in range(2):
                base = 4 * head_size * g + LANES * p
                lower = (2 * head_size - LANES) * p
                middle, upper = lower + head_size, lower + 2 * head_size
                in_a = jnp.where((lane >= lower) & (lane < middle), 1.0, 0.0)
                in_b = jnp.where((lane >= middle) & (lane < upper), 1.0, 0.0)
                query = qx[BLOCK * b : BLOCK * (b + 1), base : base + keys]
                query = jnp.concatenate(
                    [query * in_a.astype(jnp.bfloat16), query * in_b.astype(jnp.bfloat16)], axis=0
                )
                scores = dot_t(query, kvx[start : start + keys, base : base + keys]) * scale + bias
                weights = jnp.exp(scores - jnp.max(scores, axis=1, keepdims=True))
                probs = (weights / jnp.sum(weights, axis=1, keepdims=True)).astype(jnp.bfloat16)
                value = dot(
                    probs,
                    kvx[start : start + keys, head_width + base : head_width + base + keys],
                )
                pairs.append(value[:BLOCK] * in_a + value[BLOCK:] * in_b)
            joined = jnp.concatenate(
                [
                    pairs[0][:, :LANES],
                    pairs[0][:, LANES:] + pairs[1][:, :LANES],
                    pairs[1][:, LANES:],
                ],
                axis=1,
            )
            ctx[BLOCK * b : BLOCK * (b + 1), 4 * head_size * g : 4 * head_size * (g + 1)] = (
                joined.astype(jnp.bfloat16)
            )
    ctx_t[...] = ctx[ROW_PAD : ROW_PAD + rows].astype(jnp.float32).T.astype(jnp.bfloat16)

    def forward(i):
        piece = wfull.at[rows_of(from_f(i), c)]
        return copy(piece, piece, fs.at[i], fr.at[i], sib, f)

    for i in range(1, nf):
        w_copies[i - 1].wait_recv()
        forward(i).start()
    for i in range(1, nf):
        k_copies[i - 1].wait_recv()
    for s in range(nf):
        for i in range(per_shard):
            taps = kall[s, :, LANES * i : LANES * (i + 1)].astype(jnp.float32)
            for k in range(KW):
                kf[s * per_shard + i, k] = jnp.broadcast_to(taps[k : k + 1], (8, LANES))
    for i in range(1, nf):
        forward(i).wait_recv()

    for j in range(nz):
        columns = slice(chunk_w * j, chunk_w * (j + 1))
        out = inx[:, columns].astype(jnp.float32) + dot(ctx[...], wfull[:, columns])
        out = out.astype(jnp.bfloat16).astype(jnp.float32)
        for i in range(per_piece):
            res[per_piece * j + i] = out[:, LANES * i : LANES * (i + 1)]

    def tiles(x):
        return x.reshape(x.shape[0] // 8, 8, LANES)

    def conv_chunk(n, carry):
        columns = pl.ds(pl.multiple_of(n * LANES, LANES), LANES)
        part_rows = span // 2
        for h in range(2):
            lead = part_rows * h
            conv = jnp.zeros((part_rows // 8, 8, LANES), jnp.float32)
            for b in range(8):
                shifted = tiles(res[n, pl.ds(lead + b, part_rows + 24), :])
                for a in range(KW // 8):
                    k = 8 * a + b
                    mask = tiles(m1[k, lead : lead + part_rows])
                    conv = conv + mask * (kf[n, k][None] * shifted[a : a + part_rows // 8])
            conv = conv.reshape(part_rows, LANES)
            sig = jax.nn.sigmoid(conv)
            cot = cotx[lead : lead + part_rows, columns].astype(jnp.float32)
            gs[lead : lead + part_rows] = cot * sig * (1.0 + conv * (1.0 - sig))
        part_rows = rows // 2
        for h in range(2):
            lead = part_rows * h
            mid = slice(COT_PAD + lead, COT_PAD + lead + part_rows)
            back = tiles(cotx[mid, columns].astype(jnp.float32))
            for b in range(8):
                low = 8 if b == 0 else 0
                shifted = tiles(gs[lead + b + low : lead + b + low + part_rows + 24])
                for a in range(KW // 8):
                    o = 8 * a + b + low
                    mask = tiles(m1[o, mid])
                    back = back + mask * (kf[n, KW - o][None] * shifted[a : a + part_rows // 8])
            rg[lead : lead + part_rows, columns] = back.reshape(part_rows, LANES).astype(jnp.bfloat16)
        for h in range(2):
            lead = part_rows * h
            mid = slice(COT_PAD + lead, COT_PAD + lead + part_rows)
            grad = tiles(gs[mid])
            for b in range(8):
                shifted = tiles(res[n, pl.ds(COT_PAD + lead + b, part_rows + 24), :])
                for a in range(KW // 8):
                    k = 8 * a + b
                    mask = tiles(m1[k, mid])
                    prod = jnp.sum(mask * grad * shifted[a : a + part_rows // 8], axis=0)
                    if h == 0:
                        kgp[k] = prod
                    else:
                        kgs[n, k : k + 1, :] = jnp.sum(prod + kgp[k], axis=0, keepdims=True)
        return carry

    def a_copy(j):
        return copy(asrc.at[j], abuf.at[j], as_.at[j], ar.at[j], sib, f)

    def b_copy(j, i):
        return copy(
            bsrc.at[j, other_f(i)], bbuf.at[j, i], bs.at[j, i], br.at[j, i], t, other_f(i)
        )

    def c_copy(j):
        return copy(csrc.at[j], cbuf.at[z], cs.at[j], cr.at[z], 2 * j + c, f)

    def finish_a(j):
        a_copy(j).wait_recv()
        for s in range(nf):
            bsrc[j, s] = (own[j, s] + abuf[j, s].astype(jnp.float32)).astype(jnp.bfloat16)
        for i in range(1, nf):
            b_copy(j, i).start()

    def finish_b(j):
        acc = own[j, f] + abuf[j, f].astype(jnp.float32)
        for i in range(1, nf):
            b_copy(j, i).wait_recv()
            acc = acc + bbuf[j, i].astype(jnp.float32)

        @pl.when(z == j)
        def _():
            fsum[...] = acc

        @pl.when(z != j)
        def _():
            csrc[j] = acc.astype(jnp.bfloat16)
            c_copy(j).start()

    for j in range(nz):
        lax.fori_loop(per_piece * j, per_piece * (j + 1), conv_chunk, 0)
        part[...] = dot(ctx_t[...], rg[:, chunk_w * j : chunk_w * (j + 1)])
        for s in range(nf):
            own[j, s] = part[rows_of(s, c)]
            asrc[j, s] = part[rows_of(s, 1 - c)].astype(jnp.bfloat16)
        a_copy(j).start()
        if j >= 1:
            finish_a(j - 1)
        if j >= 2:
            finish_b(j - 2)

    def kb_copy(i):
        return copy(kgsrc.at[other_f(i)], kgb.at[i], kbs.at[i], kbr.at[i], t, other_f(i))

    for s in range(nf):
        for i in range(per_shard):
            kgsrc[s, i] = kgs[s * per_shard + i].astype(jnp.bfloat16)
    for i in range(1, nf):
        kb_copy(i).start()
    finish_a(nz - 1)
    if nz >= 2:
        finish_b(nz - 2)
    cg_ref[...] = dot_t(rg[...], wfull[...]).astype(jnp.bfloat16)

    kg_sum = kgs[pl.ds(f * per_shard, per_shard)]
    for i in range(1, nf):
        kb_copy(i).wait_recv()
        kg_sum = kg_sum + kgb[i].astype(jnp.float32)
    kgcs[...] = kg_sum.astype(jnp.bfloat16)

    def kc_copy(i):
        return copy(kgcs, kgc.at[z], kcs.at[i], kcr.at[z], 2 * other_z(i) + c, f)

    def kc_from(i):
        s = other_z(i)
        return copy(kgcs, kgc.at[s], kcs.at[i], kcr.at[s], 2 * s + c, f)

    for i in range(1, nz):
        kc_copy(i).start()
    kgc[z] = kgcs[...]
    finish_b(nz - 1)

    def c_from(i):
        s = other_z(i)
        return copy(csrc.at[0], cbuf.at[s], cs.at[0], cr.at[s], 2 * s + c, f)

    final = fsum[...]
    for i in range(1, nz):
        c_from(i).wait_recv()
        final = final + cbuf[other_z(i)].astype(jnp.float32)
    gbuf[c, z] = final.astype(jnp.bfloat16)

    def g_copy(i):
        piece = gbuf.at[c, z]
        return copy(piece, piece, gsn.at[i], grc.at[z], 2 * other_z(i) + c, f)

    def g_from(i):
        s = other_z(i)
        piece = gbuf.at[c, s]
        return copy(piece, piece, gsn.at[i], grc.at[s], 2 * s + c, f)

    def d_copy(s):
        piece = gbuf.at[c, s]
        return copy(piece, piece, ds_.at[s], dr.at[s], sib, f)

    def d_from(s):
        piece = gbuf.at[1 - c, s]
        return copy(piece, piece, ds_.at[s], dr.at[s], sib, f)

    for i in range(1, nz):
        g_copy(i).start()
    d_copy(z).start()

    for i in range(1, nz):
        kc_from(i).wait_recv()
    kg_z = kgc[0].astype(jnp.float32)
    for s in range(1, nz):
        kg_z = kg_z + kgc[s].astype(jnp.float32)
    kgds[...] = kg_z.astype(jnp.bfloat16)
    kd_copy = copy(kgds, kgd, kds, kdr, sib, f)
    kd_copy.start()

    for i in range(1, nz):
        g_from(i).wait_recv()
        d_copy(other_z(i)).start()
    kd_copy.wait_recv()
    kg_all = kgds[...].astype(jnp.float32) + kgd[...].astype(jnp.float32)
    for i in range(per_shard):
        kg_ref[:, LANES * i : LANES * (i + 1)] = kg_all[i]
    mine = pl.ds(pl.multiple_of(c * half, 16), half)
    theirs = pl.ds(pl.multiple_of((1 - c) * half, 16), half)
    for s in range(nz):
        wg_ref[mine, chunk_w * s : chunk_w * (s + 1)] = gbuf[c, s]
    for i in range(nz):
        d_from(other_z(i)).wait_recv()
    for s in range(nz):
        wg_ref[theirs, chunk_w * s : chunk_w * (s + 1)] = gbuf[1 - c, s]

    @pl.when(t < nt - 1)
    def _():
        for n in range(4):
            up_copy(n).wait_send()

    @pl.when(t > 0)
    def _():
        for n in range(4):
            down_copy(n).wait_send()

    for i in range(1, nf):
        w_copies[i - 1].wait_send()
        k_copies[i - 1].wait_send()
        forward(i).wait_send()
        kb_copy(i).wait_send()
    for j in range(nz):
        a_copy(j).wait_send()
        for i in range(1, nf):
            b_copy(j, i).wait_send()

        @pl.when(z != j)
        def _():
            c_copy(j).wait_send()

    for i in range(1, nz):
        kc_copy(i).wait_send()
        g_copy(i).wait_send()
    for i in range(nz):
        d_copy(other_z(i)).wait_send()
    kd_copy.wait_send()


def fused(nt, nf, queries, keys_values, inputs, cotangent, out_weight, conv_kernel, utt_starts):
    rows, head_width = queries.shape[1:]
    width = inputs.shape[2]
    nz = nt // 2
    shard = out_weight.shape[0]
    half = shard // 2
    chunks = width // LANES
    per_shard = chunks // nf
    chunk_w = width // nz
    ext = rows + 2 * ROW_PAD
    span = rows + 2 * COT_PAD
    bf16, f32 = jnp.bfloat16, jnp.float32
    dma = pltpu.SemaphoreType.DMA
    vmem = pl.BlockSpec(memory_space=pltpu.VMEM)
    scratch = [
        ((rows + 2 * KEY_PAD, 2 * head_width), bf16),
        ((ext, head_width), bf16),
        ((ext, width), bf16),
        ((span, width), bf16),
        ((head_width, width), bf16),
        ((nf, KW, width // nf), bf16),
        ((chunks, KW, 8, LANES), f32),
        ((ext, LANES), f32),
        ((KW + 1, span, LANES), f32),
        ((ext, head_width), bf16),
        ((head_width, rows), bf16),
        ((chunks, ext, LANES), f32),
        ((span, LANES), f32),
        ((rows, width), bf16),
        ((chunks, KW, LANES), f32),
        ((KW, 8, LANES), f32),
        ((head_width, chunk_w), f32),
        ((nz, nf, half, chunk_w), f32),
        ((nz, nf, half, chunk_w), bf16),
        ((nz, nf, half, chunk_w), bf16),
        ((nz, nf, half, chunk_w), bf16),
        ((nz, nf, half, chunk_w), bf16),
        ((half, chunk_w), f32),
        ((nz, half, chunk_w), bf16),
        ((nz, half, chunk_w), bf16),
        ((2, nz, half, chunk_w), bf16),
        ((nf, per_shard, KW, LANES), bf16),
        ((nf, per_shard, KW, LANES), bf16),
        ((per_shard, KW, LANES), bf16),
        ((nz, per_shard, KW, LANES), bf16),
        ((per_shard, KW, LANES), bf16),
        ((per_shard, KW, LANES), bf16),
    ]
    sems = [
        (6,), (2, 4), (2, 4), (nf,), (nf,), (nf,), (nf,), (nf,), (nf,), (nz,), (nz,), (nz, nf), (nz, nf),
        (nz,), (nz,), (nz,), (nz,), (nz,), (nz,), (nf,), (nf,), (nz,), (nz,),
    ]
    context_grad, weight_grad, kernel_grad = pl.pallas_call(
        functools.partial(block_kernel, nt, nf),
        out_shape=(
            jax.ShapeDtypeStruct((rows, head_width), bf16),
            jax.ShapeDtypeStruct((shard, width), bf16),
            jax.ShapeDtypeStruct((KW, width // nf), f32),
        ),
        in_specs=[pl.BlockSpec(memory_space=pltpu.SMEM)] + [pl.BlockSpec(memory_space=pltpu.HBM)] * 6,
        out_specs=(vmem, vmem, vmem),
        scratch_shapes=[pltpu.VMEM(*s) for s in scratch]
        + [dma(s) for s in sems]
        + [dma, dma],
        compiler_params=pltpu.CompilerParams(
            collective_id=0, has_side_effects=True, vmem_limit_bytes=48 * 1024 * 1024
        ),
    )(utt_starts, queries[0], keys_values[0], inputs[0], cotangent[0], out_weight, conv_kernel)
    grad_scale = 1.0 / math.sqrt(nf * queries.shape[0] * nt * rows)
    return (
        context_grad[None],
        weight_grad.astype(jnp.float32) * grad_scale,
        kernel_grad * grad_scale,
    )


def fits(nt, nf, queries, keys_values, inputs, cotangent, out_weight, conv_kernel, utt_starts):
    rows, head_width = queries.shape[1:]
    width = inputs.shape[2]
    return (
        queries.shape[0] == 1
        and rows == 2 * BLOCK
        and nt % 2 == 0
        and nt >= 4
        and (width // LANES) % (nt // 2) == 0
        and (width // LANES) % nf == 0
        and out_weight.shape[0] % 32 == 0
        and head_width * LANES == HEADS_W * 96 * LANES
    )


def solution(mesh):
    nt, nf = mesh.shape["tm"], mesh.shape["fsdp"]

    def body(*arrays):
        if fits(nt, nf, *arrays):
            return fused(nt, nf, *arrays)
        return shards(*arrays)

    return jax.shard_map(
        body,
        mesh=mesh,
        in_specs=(
            P("fsdp", "tm", None),
            P("fsdp", "tm", None),
            P("fsdp", "tm", None),
            P("fsdp", "tm", None),
            P("fsdp", None),
            P(None, "fsdp"),
            P("fsdp", None),
        ),
        out_specs=(P("fsdp", "tm", None), P("fsdp", None), P(None, "fsdp")),
        check_vma=False,
    )
```

```python
import functools
import math

import jax
import jax.numpy as jnp
from jax import lax
from jax.experimental import pallas as pl
from jax.experimental.pallas import tpu as pltpu
from jax.sharding import PartitionSpec as P

HEADS_W = 8
KW = 32
WIN = 128


masked_score = -1e30


def with_halo(x, sides, width):
    for axis, dim in sides:
        devices, length = (lax.axis_size(axis), x.shape[dim])
        up = [(i, (i + 1) % devices) for i in range(devices - 1)]
        down = [(j, i) for i, j in up]
        last = lax.slice_in_dim(x, length - width, length, axis=dim)
        initial = lax.slice_in_dim(x, 0, width, axis=dim)
        before = lax.ppermute(last, axis, up)
        after = lax.ppermute(initial, axis, down)
        x = jnp.concatenate([before, x, after], axis=dim)
    return x


def segment_ids(starts_row, positions):
    return jnp.sum((starts_row[None, :] <= positions[:, None]).astype(jnp.int32), axis=1) - 1


def shards(queries, keys_values, inputs, cotangent, out_weight, conv_kernel, utt_starts):
    query_rows = queries[0]
    kv_rows = keys_values[0]
    input_rows = inputs[0]
    cotangent_rows = cotangent[0]
    starts_row = utt_starts[0]
    local_frames = query_rows.shape[0]
    head_width = query_rows.shape[1]
    head_size = head_width // HEADS_W
    window_half = WIN // 2
    conv_reach = KW - 1
    conv_lead = KW // 2
    conv_span = local_frames + KW - 1
    frames_total = local_frames * lax.axis_size("tm")
    first_frame = lax.axis_index("tm") * local_frames
    full_weight, full_kernel = (
        lax.all_gather(out_weight, "fsdp", axis=0, tiled=True),
        lax.all_gather(conv_kernel, "fsdp", axis=1, tiled=True),
    )
    kv_ext = with_halo(kv_rows, (("tm", 0),), window_half)
    key_span = local_frames + 2 * window_half
    key_positions = first_frame - window_half + jnp.arange(key_span, dtype=jnp.int32)
    key_seg = jnp.where(key_positions < frames_total, segment_ids(starts_row, key_positions), -1)
    query_seg = segment_ids(starts_row, first_frame + jnp.arange(local_frames, dtype=jnp.int32))
    key_offset = (
        jnp.arange(key_span, dtype=jnp.int32)[None, :]
        - jnp.arange(local_frames, dtype=jnp.int32)[:, None]
    )
    allowed = (
        (key_offset >= 0)
        & (key_offset <= 2 * window_half)
        & (query_seg[:, None] == key_seg[None, :])
    )
    query_heads = query_rows.reshape(local_frames, HEADS_W, head_size)
    key_heads = kv_ext[:, :head_width].reshape(key_span, HEADS_W, head_size)
    value_heads = kv_ext[:, head_width:].reshape(key_span, HEADS_W, head_size)
    scores = jnp.einsum(
        "qhe,khe->hqk", query_heads, key_heads, preferred_element_type=jnp.float32
    ) / math.sqrt(head_size)
    scores = jnp.where(allowed[None], scores, masked_score)
    row_max = jnp.max(scores, axis=2, keepdims=True)
    exp_scores = jnp.exp(scores - row_max)
    attn_probs = (exp_scores / jnp.sum(exp_scores, axis=2, keepdims=True)).astype(jnp.bfloat16)
    context = jnp.einsum(
        "hqk,khe->qhe", attn_probs, value_heads, preferred_element_type=jnp.float32
    )
    context = context.reshape(local_frames, head_width).astype(jnp.bfloat16)
    residual = (
        input_rows.astype(jnp.float32)
        + jnp.dot(context, full_weight, preferred_element_type=jnp.float32)
    ).astype(jnp.bfloat16)
    stacked_rims = with_halo(jnp.stack([residual, cotangent_rows]), (("tm", 1),), conv_reach)
    residual_ext = stacked_rims[0]
    cotangent_ext = stacked_rims[1][conv_lead : conv_lead + conv_span]
    residual_positions = (
        first_frame - conv_reach + jnp.arange(local_frames + 2 * conv_reach, dtype=jnp.int32)
    )
    residual_seg = segment_ids(starts_row, residual_positions)
    conv_seg = residual_seg[conv_lead : conv_lead + conv_span]
    own_seg = residual_seg[conv_reach : conv_reach + local_frames]
    kernel_float = full_kernel.astype(jnp.float32)
    conv_out = jnp.zeros((conv_span, residual.shape[1]), jnp.float32)
    for offset in range(KW):
        same_utt = (conv_seg == residual_seg[offset : offset + conv_span])[:, None]
        conv_out = conv_out + jnp.where(
            same_utt,
            kernel_float[offset] * residual_ext[offset : offset + conv_span].astype(jnp.float32),
            0.0,
        )
    gate_sig = jax.nn.sigmoid(conv_out)
    gated_grad = cotangent_ext.astype(jnp.float32) * gate_sig * (1.0 + conv_out * (1.0 - gate_sig))
    back_sum = cotangent_rows.astype(jnp.float32)
    own_lower = conv_lead - 1
    own_grad = gated_grad[own_lower : own_lower + local_frames]
    own_conv_seg = conv_seg[own_lower : own_lower + local_frames]
    for offset in range(KW):
        lower = KW - 1 - offset
        same_back = (conv_seg[lower : lower + local_frames] == own_seg)[:, None]
        back_sum = back_sum + jnp.where(
            same_back, kernel_float[offset] * gated_grad[lower : lower + local_frames], 0.0
        )
    products = jnp.stack(
        [
            jnp.where(
                (
                    own_conv_seg
                    == residual_seg[own_lower + offset : own_lower + offset + local_frames]
                )[:, None],
                own_grad
                * residual_ext[own_lower + offset : own_lower + offset + local_frames].astype(
                    jnp.float32
                ),
                0.0,
            )
            for offset in range(KW)
        ]
    )
    kernel_part = jnp.sum(products, axis=1)
    residual_grad = back_sum.astype(jnp.bfloat16)
    context_grad = lax.dot_general(
        residual_grad, full_weight, (((1,), (1,)), ((), ())), preferred_element_type=jnp.float32
    ).astype(jnp.bfloat16)
    grad_scale = 1.0 / math.sqrt(lax.axis_size("fsdp") * queries.shape[0] * frames_total)
    weight_part = (
        lax.dot_general(
            context, residual_grad, (((0,), (0,)), ((), ())), preferred_element_type=jnp.float32
        )
        * grad_scale
    )
    weight_share, kernel_share = (
        lax.psum_scatter(
            weight_part.astype(jnp.bfloat16), "fsdp", scatter_dimension=0, tiled=True
        ).astype(jnp.float32),
        lax.psum_scatter(
            (kernel_part * grad_scale).astype(jnp.bfloat16), "fsdp", scatter_dimension=1, tiled=True
        ).astype(jnp.float32),
    )
    weight_grad, kernel_grad = lax.psum((weight_share, kernel_share), "tm")
    return (context_grad[None], weight_grad, kernel_grad)


MESH = pl.DeviceIdType.MESH
KEY_PAD = 96
ROW_PAD = 32
COT_PAD = 16
GROUP = 32
BLOCK = 64
LANES = 128


def dot(a, b):
    return jnp.dot(a, b, preferred_element_type=jnp.float32)


def dot_t(a, b):
    return lax.dot_general(a, b, (((1,), (1,)), ((), ())), preferred_element_type=jnp.float32)


def block_kernel(
    nt, nf,
    starts_ref, q_ref, kv_ref, in_ref, cot_ref, w_ref, ck_ref,
    cg_ref, wg_ref, kg_ref,
    kvx, qx, inx, cotx, wfull, kall, kf, seg, m1, ctx, ctx_t, res, gs, rg, kgs, kgp, ms,
    part, own, asrc, abuf, bsrc, bbuf, fsum, csrc, cbuf, gbuf,
    kgsrc, kgb, kgcs, kgc, kgds, kgd,
    ls, hs, hr, ws, wr, fs, fr, ks, kr, as_, ar, bs, br, cs, cr, gsn, grc, ds_, dr,
    kbs, kbr, kcs, kcr, kds, kdr,
):
    nz = nt // 2
    t = lax.axis_index("tm")
    f = lax.axis_index("fsdp")
    z = lax.div(t, 2)
    c = lax.rem(t, 2)
    sib = t + 1 - 2 * c
    rows = q_ref.shape[0]
    shard = w_ref.shape[0]
    half = shard // 2
    width = in_ref.shape[1]
    head_width = q_ref.shape[1]
    head_size = head_width // HEADS_W
    chunks = width // LANES
    per_shard = chunks // nf
    chunk_w = width // nz
    per_piece = chunks // nz
    ext = rows + 2 * ROW_PAD
    span = rows + 2 * COT_PAD
    first = t * rows
    total = nt * rows

    def other_f(i):
        return lax.rem(f + i, nf)

    def from_f(i):
        return lax.rem(f + nf - i, nf)

    def other_z(i):
        return lax.rem(z + i, nz)

    def copy(src, dst, send, recv, tm, fsdp):
        return pltpu.make_async_remote_copy(
            src_ref=src, dst_ref=dst, send_sem=send, recv_sem=recv,
            device_id={"tm": tm, "fsdp": fsdp}, device_id_type=MESH,
        )

    halo = ((kv_ref, kvx, KEY_PAD), (q_ref, qx, ROW_PAD), (in_ref, inx, ROW_PAD), (cot_ref, cotx, COT_PAD))
    own_copies = [
        pltpu.make_async_copy(src, dst.at[pl.ds(pad, rows)], ls.at[n])
        for n, (src, dst, pad) in enumerate(halo)
    ]
    own_copies.append(
        pltpu.make_async_copy(
            w_ref, wfull.at[pl.ds(pl.multiple_of(f * shard, 16), shard)], ls.at[4]
        )
    )
    own_copies.append(pltpu.make_async_copy(ck_ref, kall.at[f], ls.at[5]))
    for own_copy in own_copies:
        own_copy.start()

    barrier = pltpu.get_barrier_semaphore()

    def greet(tm, fsdp):
        pl.semaphore_signal(
            barrier, inc=1, device_id={"tm": tm, "fsdp": fsdp}, device_id_type=MESH
        )

    for i in range(1, nf):
        greet(t, other_f(i))
    for i in range(1, nz):
        greet(2 * other_z(i) + c, f)

    @pl.when(t > 0)
    def _():
        greet(t - 1, f)

    @pl.when(t < nt - 1)
    def _():
        greet(t + 1, f)

    near = jnp.minimum(t, 1) + jnp.minimum(nt - 1 - t, 1)
    pl.semaphore_wait(barrier, nf - 1 + nz - 1 + near)

    def up_copy(n):
        src, dst, pad = halo[n]
        return copy(
            src.at[pl.ds(rows - pad, pad)], dst.at[pl.ds(0, pad)], hs.at[0, n], hr.at[0, n], t + 1, f
        )

    def down_copy(n):
        src, dst, pad = halo[n]
        return copy(
            src.at[pl.ds(0, pad)], dst.at[pl.ds(pad + rows, pad)], hs.at[1, n], hr.at[1, n], t - 1, f
        )

    @pl.when(t < nt - 1)
    def _():
        for n in range(4):
            up_copy(n).start()

    @pl.when(t > 0)
    def _():
        for n in range(4):
            down_copy(n).start()

    def rows_of(owner, core):
        return pl.ds(pl.multiple_of(owner * shard + core * half, 16), half)

    def cols(j):
        return pl.ds(chunk_w * j, chunk_w)

    def w_copy(j, i):
        return copy(
            w_ref.at[pl.ds(pl.multiple_of(c * half, 16), half), cols(j)],
            wfull.at[rows_of(f, c), cols(j)], ws.at[j, i], wr.at[j, i], t, other_f(i),
        )

    k_copies = [
        copy(ck_ref, kall.at[f], ks.at[i], kr.at[i], t, other_f(i)) for i in range(1, nf)
    ]
    for k_copy in k_copies:
        k_copy.start()
    for j in range(nz):
        for i in range(1, nf):
            w_copy(j, i).start()

    @pl.when(t == 0)
    def _():
        for src, dst, pad in halo:
            dst[0:pad] = jnp.zeros((pad, dst.shape[1]), dst.dtype)

    @pl.when(t == nt - 1)
    def _():
        for src, dst, pad in halo:
            dst[pad + rows : 2 * pad + rows] = jnp.zeros((pad, dst.shape[1]), dst.dtype)


    utts = starts_ref.shape[1]

    def segments(positions):
        found = jnp.full(positions.shape, -1.0, jnp.float32)
        for u in range(utts):
            found = found + jnp.where(starts_ref[0, u] <= positions, 1.0, 0.0)
        return jnp.where(positions < total, found, -1.0)

    seg[...] = segments(lax.broadcasted_iota(jnp.int32, (ext, LANES), 0) + (first - ROW_PAD))

    for k in range(KW + 1):
        m1[k] = jnp.where(seg[k : k + span] == seg[COT_PAD : COT_PAD + span], 1.0, 0.0)

    @pl.when(t > 0)
    def _():
        for n in range(4):
            up_copy(n).wait_recv()

    @pl.when(t < nt - 1)
    def _():
        for n in range(4):
            down_copy(n).wait_recv()

    for own_copy in own_copies:
        own_copy.wait()

    keys = 2 * LANES
    key_rows = rows + 2 * KEY_PAD
    scale = 1.0 / math.sqrt(head_size)
    lane = lax.broadcasted_iota(jnp.int32, (1, keys), 1)
    for b in range(ext // BLOCK):
        start = min(BLOCK * b, key_rows - keys)
        key_seg = segments(lane + (first - KEY_PAD + start))
        query_seg = seg[BLOCK * b : BLOCK * (b + 1)]
        query_seg = jnp.concatenate([query_seg, query_seg], axis=1)
        gap = (
            lax.broadcasted_iota(jnp.int32, (BLOCK, keys), 1)
            - lax.broadcasted_iota(jnp.int32, (BLOCK, keys), 0)
            + (start - KEY_PAD - BLOCK * b + ROW_PAD)
        )
        allowed = (gap >= -(WIN // 2)) & (gap <= WIN // 2) & (query_seg == key_seg)
        bias = jnp.where(allowed, 0.0, masked_score)
        bias = jnp.concatenate([bias, bias], axis=0)
        for g in range(HEADS_W // 4):
            pairs = []
            for p in range(2):
                base = 4 * head_size * g + LANES * p
                lower = (2 * head_size - LANES) * p
                middle, upper = lower + head_size, lower + 2 * head_size
                in_a = jnp.where((lane >= lower) & (lane < middle), 1.0, 0.0)
                in_b = jnp.where((lane >= middle) & (lane < upper), 1.0, 0.0)
                query = qx[BLOCK * b : BLOCK * (b + 1), base : base + keys]
                query = jnp.concatenate(
                    [query * in_a.astype(jnp.bfloat16), query * in_b.astype(jnp.bfloat16)], axis=0
                )
                scores = dot_t(query, kvx[start : start + keys, base : base + keys]) * scale + bias
                weights = jnp.exp(scores - jnp.max(scores, axis=1, keepdims=True))
                probs = (weights / jnp.sum(weights, axis=1, keepdims=True)).astype(jnp.bfloat16)
                value = dot(
                    probs,
                    kvx[start : start + keys, head_width + base : head_width + base + keys],
                )
                pairs.append(value[:BLOCK] * in_a + value[BLOCK:] * in_b)
            joined = jnp.concatenate(
                [
                    pairs[0][:, :LANES],
                    pairs[0][:, LANES:] + pairs[1][:, :LANES],
                    pairs[1][:, LANES:],
                ],
                axis=1,
            )
            ctx[BLOCK * b : BLOCK * (b + 1), 4 * head_size * g : 4 * head_size * (g + 1)] = (
                joined.astype(jnp.bfloat16)
            )
    ctx_t[...] = ctx[ROW_PAD : ROW_PAD + rows].astype(jnp.float32).T.astype(jnp.bfloat16)

    def forward(j, i):
        piece = wfull.at[rows_of(from_f(i), c), cols(j)]
        return copy(piece, piece, fs.at[j, i], fr.at[j, i], sib, f)

    def pass_on(j):
        for i in range(1, nf):
            w_copy(j, i).wait_recv()
            forward(j, i).start()

    pass_on(0)
    for i in range(1, nf):
        k_copies[i - 1].wait_recv()
    for s in range(nf):
        for i in range(per_shard):
            taps = kall[s, :, LANES * i : LANES * (i + 1)].astype(jnp.float32)
            for k in range(KW):
                kf[s * per_shard + i, k] = jnp.broadcast_to(taps[k : k + 1], (8, LANES))
    def project(j):
        for i in range(1, nf):
            forward(j, i).wait_recv()
        columns = slice(chunk_w * j, chunk_w * (j + 1))
        out = inx[:, columns].astype(jnp.float32) + dot(ctx[...], wfull[:, columns])
        out = out.astype(jnp.bfloat16).astype(jnp.float32)
        for i in range(per_piece):
            res[per_piece * j + i] = out[:, LANES * i : LANES * (i + 1)]

    def tiles(x):
        return x.reshape(x.shape[:-2] + (x.shape[-2] // 8, 8, LANES))

    def conv_group(j):
        lanes = slice(per_piece * j, per_piece * (j + 1))

        def cot_rows(lead):
            return jnp.stack(
                [
                    cotx[lead : lead + GROUP, LANES * n : LANES * (n + 1)].astype(jnp.float32)
                    for n in range(per_piece * j, per_piece * (j + 1))
                ]
            )

        for lead in range(0, span, GROUP):
            conv = jnp.zeros((per_piece, GROUP // 8, 8, LANES), jnp.float32)
            for b in range(8):
                shifted = tiles(res[lanes, lead + b : lead + b + GROUP + 24, :])
                for a in range(KW // 8):
                    k = 8 * a + b
                    mask = tiles(m1[k, lead : lead + GROUP])
                    kept = mask[None] * shifted[:, a : a + GROUP // 8]
                    ms[k, :, lead : lead + GROUP] = kept.reshape(per_piece, GROUP, LANES)
                    conv = conv + kf[lanes, k][:, None] * kept
            conv = conv.reshape(per_piece, GROUP, LANES)
            sig = jax.nn.sigmoid(conv)
            gs[:, lead : lead + GROUP] = cot_rows(lead) * sig * (1.0 + conv * (1.0 - sig))
        for lead in range(0, rows, GROUP):
            mid = slice(COT_PAD + lead, COT_PAD + lead + GROUP)
            back = tiles(cot_rows(COT_PAD + lead))
            for b in range(8):
                low = 8 if b == 0 else 0
                shifted = tiles(gs[:, lead + b + low : lead + b + low + GROUP + 24])
                for a in range(KW // 8):
                    o = 8 * a + b + low
                    mask = tiles(m1[o, mid])
                    back = back + mask[None] * (
                        kf[lanes, KW - o][:, None] * shifted[:, a : a + GROUP // 8]
                    )
            back = back.reshape(per_piece, GROUP, LANES).astype(jnp.bfloat16)
            for i in range(per_piece):
                n = per_piece * j + i
                rg[lead : lead + GROUP, LANES * n : LANES * (n + 1)] = back[i]
        for lead in range(0, rows, 2 * GROUP):
            mid = slice(COT_PAD + lead, COT_PAD + lead + 2 * GROUP)
            grad = tiles(gs[:, mid])
            for k in range(KW):
                prod = jnp.sum(grad * tiles(ms[k, :, mid]), axis=1)
                kgp[k] = prod if lead == 0 else prod + kgp[k]
        for i in range(per_piece):
            kgs[per_piece * j + i] = jnp.sum(kgp[:, i], axis=1)

    def a_copy(j):
        return copy(asrc.at[j], abuf.at[j], as_.at[j], ar.at[j], sib, f)

    def b_copy(j, i):
        return copy(
            bsrc.at[j, other_f(i)], bbuf.at[j, i], bs.at[j, i], br.at[j, i], t, other_f(i)
        )

    owners = sorted(range(nz), key=lambda s: -abs(2 * s - nz + 1))

    def c_copy(j):
        return copy(csrc.at[j], cbuf.at[z], cs.at[j], cr.at[z], 2 * owners[j] + c, f)

    def c_from(i):
        s = other_z(i)
        return copy(csrc.at[0], cbuf.at[s], cs.at[0], cr.at[s], 2 * s + c, f)

    def g_copy(j, i):
        piece = gbuf.at[c, j]
        return copy(piece, piece, gsn.at[i], grc.at[j], 2 * other_z(i) + c, f)

    def d_copy(j):
        piece = gbuf.at[c, j]
        return copy(piece, piece, ds_.at[j], dr.at[j], sib, f)

    def d_from(j):
        piece = gbuf.at[1 - c, j]
        return copy(piece, piece, ds_.at[j], dr.at[j], sib, f)

    def finish_c(j):
        @pl.when(z == owners[j])
        def _():
            final = fsum[...]
            for i in range(1, nz):
                c_from(i).wait_recv()
                final = final + cbuf[other_z(i)].astype(jnp.float32)
            gbuf[c, j] = final.astype(jnp.bfloat16)
            for i in range(1, nz):
                g_copy(j, i).start()
            d_copy(j).start()

    def take(j):
        @pl.when(z != owners[j])
        def _():
            g_copy(j, 1).wait_recv()
            d_copy(j).start()

    def finish_a(j):
        a_copy(j).wait_recv()
        for s in range(nf):
            bsrc[j, s] = (own[j, s] + abuf[j, s].astype(jnp.float32)).astype(jnp.bfloat16)
        for i in range(1, nf):
            b_copy(j, i).start()

    def finish_b(j):
        acc = own[j, f] + abuf[j, f].astype(jnp.float32)
        for i in range(1, nf):
            b_copy(j, i).wait_recv()
            acc = acc + bbuf[j, i].astype(jnp.float32)

        @pl.when(z == owners[j])
        def _():
            fsum[...] = acc

        @pl.when(z != owners[j])
        def _():
            csrc[j] = acc.astype(jnp.bfloat16)
            c_copy(j).start()

    for j in range(nz):
        project(j)
        if j + 1 < nz:
            pass_on(j + 1)
        conv_group(j)
        part[...] = dot(ctx_t[...], rg[:, chunk_w * j : chunk_w * (j + 1)])
        for s in range(nf):
            own[j, s] = part[rows_of(s, c)]
            asrc[j, s] = part[rows_of(s, 1 - c)].astype(jnp.bfloat16)
        a_copy(j).start()
        if j >= 1:
            finish_a(j - 1)
        if j >= 2:
            finish_b(j - 2)
        if j >= 3:
            finish_c(j - 3)

    def kb_copy(i):
        return copy(kgsrc.at[other_f(i)], kgb.at[i], kbs.at[i], kbr.at[i], t, other_f(i))

    for s in range(nf):
        for i in range(per_shard):
            kgsrc[s, i] = kgs[s * per_shard + i].astype(jnp.bfloat16)
    for i in range(1, nf):
        kb_copy(i).start()
    finish_a(nz - 1)
    if nz >= 2:
        finish_b(nz - 2)
    if nz >= 3:
        finish_c(nz - 3)
    cg_ref[...] = dot_t(rg[...], wfull[...]).astype(jnp.bfloat16)

    kg_sum = kgs[pl.ds(f * per_shard, per_shard)]
    for i in range(1, nf):
        kb_copy(i).wait_recv()
        kg_sum = kg_sum + kgb[i].astype(jnp.float32)
    kgcs[...] = kg_sum.astype(jnp.bfloat16)

    def kc_copy(i):
        return copy(kgcs, kgc.at[z], kcs.at[i], kcr.at[z], 2 * other_z(i) + c, f)

    def kc_from(i):
        s = other_z(i)
        return copy(kgcs, kgc.at[s], kcs.at[i], kcr.at[s], 2 * s + c, f)

    for i in range(1, nz):
        kc_copy(i).start()
    kgc[z] = kgcs[...]
    finish_b(nz - 1)

    if nz >= 2:
        finish_c(nz - 2)
    for j in range(nz - 2):
        take(j)
    finish_c(nz - 1)

    for i in range(1, nz):
        kc_from(i).wait_recv()
    kg_z = kgc[0].astype(jnp.float32)
    for s in range(1, nz):
        kg_z = kg_z + kgc[s].astype(jnp.float32)
    kgds[...] = kg_z.astype(jnp.bfloat16)
    kd_copy = copy(kgds, kgd, kds, kdr, sib, f)
    kd_copy.start()

    for j in range(max(nz - 2, 0), nz):
        take(j)
    kd_copy.wait_recv()
    kg_all = kgds[...].astype(jnp.float32) + kgd[...].astype(jnp.float32)
    for i in range(per_shard):
        kg_ref[:, LANES * i : LANES * (i + 1)] = kg_all[i]
    mine = pl.ds(pl.multiple_of(c * half, 16), half)
    theirs = pl.ds(pl.multiple_of((1 - c) * half, 16), half)
    for s in range(nz):
        wg_ref[mine, chunk_w * s : chunk_w * (s + 1)] = gbuf[c, s]
    for s in range(nz):
        d_from(s).wait_recv()
        wg_ref[theirs, chunk_w * s : chunk_w * (s + 1)] = gbuf[1 - c, s]

    @pl.when(t < nt - 1)
    def _():
        for n in range(4):
            up_copy(n).wait_send()

    @pl.when(t > 0)
    def _():
        for n in range(4):
            down_copy(n).wait_send()

    for i in range(1, nf):
        k_copies[i - 1].wait_send()
        kb_copy(i).wait_send()
    for j in range(nz):
        a_copy(j).wait_send()
        for i in range(1, nf):
            w_copy(j, i).wait_send()
            forward(j, i).wait_send()
            b_copy(j, i).wait_send()

        @pl.when(z != owners[j])
        def _():
            c_copy(j).wait_send()

    for i in range(1, nz):
        kc_copy(i).wait_send()
        g_copy(0, i).wait_send()
    for j in range(nz):
        d_copy(j).wait_send()
    kd_copy.wait_send()


def fused(nt, nf, queries, keys_values, inputs, cotangent, out_weight, conv_kernel, utt_starts):
    rows, head_width = queries.shape[1:]
    width = inputs.shape[2]
    nz = nt // 2
    shard = out_weight.shape[0]
    half = shard // 2
    chunks = width // LANES
    per_shard = chunks // nf
    chunk_w = width // nz
    per_piece = chunks // nz
    ext = rows + 2 * ROW_PAD
    span = rows + 2 * COT_PAD
    bf16, f32 = jnp.bfloat16, jnp.float32
    dma = pltpu.SemaphoreType.DMA
    vmem = pl.BlockSpec(memory_space=pltpu.VMEM)
    scratch = [
        ((rows + 2 * KEY_PAD, 2 * head_width), bf16),
        ((ext, head_width), bf16),
        ((ext, width), bf16),
        ((span, width), bf16),
        ((head_width, width), bf16),
        ((nf, KW, width // nf), bf16),
        ((chunks, KW, 8, LANES), f32),
        ((ext, LANES), f32),
        ((KW + 1, span, LANES), f32),
        ((ext, head_width), bf16),
        ((head_width, rows), bf16),
        ((chunks, ext, LANES), f32),
        ((per_piece, span, LANES), f32),
        ((rows, width), bf16),
        ((chunks, KW, LANES), f32),
        ((KW, per_piece, 8, LANES), f32),
        ((KW, per_piece, span, LANES), f32),
        ((head_width, chunk_w), f32),
        ((nz, nf, half, chunk_w), f32),
        ((nz, nf, half, chunk_w), bf16),
        ((nz, nf, half, chunk_w), bf16),
        ((nz, nf, half, chunk_w), bf16),
        ((nz, nf, half, chunk_w), bf16),
        ((half, chunk_w), f32),
        ((nz, half, chunk_w), bf16),
        ((nz, half, chunk_w), bf16),
        ((2, nz, half, chunk_w), bf16),
        ((nf, per_shard, KW, LANES), bf16),
        ((nf, per_shard, KW, LANES), bf16),
        ((per_shard, KW, LANES), bf16),
        ((nz, per_shard, KW, LANES), bf16),
        ((per_shard, KW, LANES), bf16),
        ((per_shard, KW, LANES), bf16),
    ]
    sems = [
        (6,), (2, 4), (2, 4), (nz, nf), (nz, nf), (nz, nf), (nz, nf), (nf,), (nf,), (nz,), (nz,), (nz, nf), (nz, nf),
        (nz,), (nz,), (nz,), (nz,), (nz,), (nz,), (nf,), (nf,), (nz,), (nz,),
    ]
    context_grad, weight_grad, kernel_grad = pl.pallas_call(
        functools.partial(block_kernel, nt, nf),
        out_shape=(
            jax.ShapeDtypeStruct((rows, head_width), bf16),
            jax.ShapeDtypeStruct((shard, width), bf16),
            jax.ShapeDtypeStruct((KW, width // nf), f32),
        ),
        in_specs=[pl.BlockSpec(memory_space=pltpu.SMEM)] + [pl.BlockSpec(memory_space=pltpu.HBM)] * 6,
        out_specs=(vmem, vmem, vmem),
        scratch_shapes=[pltpu.VMEM(*s) for s in scratch]
        + [dma(s) for s in sems]
        + [dma, dma],
        compiler_params=pltpu.CompilerParams(
            collective_id=0, has_side_effects=True, vmem_limit_bytes=60 * 1024 * 1024
        ),
    )(utt_starts, queries[0], keys_values[0], inputs[0], cotangent[0], out_weight, conv_kernel)
    grad_scale = 1.0 / math.sqrt(nf * queries.shape[0] * nt * rows)
    return (
        context_grad[None],
        weight_grad.astype(jnp.float32) * grad_scale,
        kernel_grad * grad_scale,
    )


def fits(nt, nf, queries, keys_values, inputs, cotangent, out_weight, conv_kernel, utt_starts):
    rows, head_width = queries.shape[1:]
    width = inputs.shape[2]
    return (
        queries.shape[0] == 1
        and rows == 2 * BLOCK
        and nt % 2 == 0
        and nt >= 4
        and (width // LANES) % (nt // 2) == 0
        and (width // LANES) % nf == 0
        and out_weight.shape[0] % 32 == 0
        and head_width * LANES == HEADS_W * 96 * LANES
    )


def solution(mesh):
    nt, nf = mesh.shape["tm"], mesh.shape["fsdp"]

    def body(*arrays):
        if fits(nt, nf, *arrays):
            return fused(nt, nf, *arrays)
        return shards(*arrays)

    return jax.shard_map(
        body,
        mesh=mesh,
        in_specs=(
            P("fsdp", "tm", None),
            P("fsdp", "tm", None),
            P("fsdp", "tm", None),
            P("fsdp", "tm", None),
            P("fsdp", None),
            P(None, "fsdp"),
            P("fsdp", None),
        ),
        out_specs=(P("fsdp", "tm", None), P("fsdp", None), P(None, "fsdp")),
        check_vma=False,
    )
```

```python
import functools
import math

import jax
import jax.numpy as jnp
from jax import lax
from jax.experimental import pallas as pl
from jax.experimental.pallas import tpu as pltpu
from jax.sharding import PartitionSpec as P

HEADS_W = 8
KW = 32
WIN = 128


masked_score = -1e30


def with_halo(x, sides, width):
    for axis, dim in sides:
        devices, length = (lax.axis_size(axis), x.shape[dim])
        up = [(i, (i + 1) % devices) for i in range(devices - 1)]
        down = [(j, i) for i, j in up]
        last = lax.slice_in_dim(x, length - width, length, axis=dim)
        initial = lax.slice_in_dim(x, 0, width, axis=dim)
        before = lax.ppermute(last, axis, up)
        after = lax.ppermute(initial, axis, down)
        x = jnp.concatenate([before, x, after], axis=dim)
    return x


def segment_ids(starts_row, positions):
    return jnp.sum((starts_row[None, :] <= positions[:, None]).astype(jnp.int32), axis=1) - 1


def shards(queries, keys_values, inputs, cotangent, out_weight, conv_kernel, utt_starts):
    query_rows = queries[0]
    kv_rows = keys_values[0]
    input_rows = inputs[0]
    cotangent_rows = cotangent[0]
    starts_row = utt_starts[0]
    local_frames = query_rows.shape[0]
    head_width = query_rows.shape[1]
    head_size = head_width // HEADS_W
    window_half = WIN // 2
    conv_reach = KW - 1
    conv_lead = KW // 2
    conv_span = local_frames + KW - 1
    frames_total = local_frames * lax.axis_size("tm")
    first_frame = lax.axis_index("tm") * local_frames
    full_weight, full_kernel = (
        lax.all_gather(out_weight, "fsdp", axis=0, tiled=True),
        lax.all_gather(conv_kernel, "fsdp", axis=1, tiled=True),
    )
    kv_ext = with_halo(kv_rows, (("tm", 0),), window_half)
    key_span = local_frames + 2 * window_half
    key_positions = first_frame - window_half + jnp.arange(key_span, dtype=jnp.int32)
    key_seg = jnp.where(key_positions < frames_total, segment_ids(starts_row, key_positions), -1)
    query_seg = segment_ids(starts_row, first_frame + jnp.arange(local_frames, dtype=jnp.int32))
    key_offset = (
        jnp.arange(key_span, dtype=jnp.int32)[None, :]
        - jnp.arange(local_frames, dtype=jnp.int32)[:, None]
    )
    allowed = (
        (key_offset >= 0)
        & (key_offset <= 2 * window_half)
        & (query_seg[:, None] == key_seg[None, :])
    )
    query_heads = query_rows.reshape(local_frames, HEADS_W, head_size)
    key_heads = kv_ext[:, :head_width].reshape(key_span, HEADS_W, head_size)
    value_heads = kv_ext[:, head_width:].reshape(key_span, HEADS_W, head_size)
    scores = jnp.einsum(
        "qhe,khe->hqk", query_heads, key_heads, preferred_element_type=jnp.float32
    ) / math.sqrt(head_size)
    scores = jnp.where(allowed[None], scores, masked_score)
    row_max = jnp.max(scores, axis=2, keepdims=True)
    exp_scores = jnp.exp(scores - row_max)
    attn_probs = (exp_scores / jnp.sum(exp_scores, axis=2, keepdims=True)).astype(jnp.bfloat16)
    context = jnp.einsum(
        "hqk,khe->qhe", attn_probs, value_heads, preferred_element_type=jnp.float32
    )
    context = context.reshape(local_frames, head_width).astype(jnp.bfloat16)
    residual = (
        input_rows.astype(jnp.float32)
        + jnp.dot(context, full_weight, preferred_element_type=jnp.float32)
    ).astype(jnp.bfloat16)
    stacked_rims = with_halo(jnp.stack([residual, cotangent_rows]), (("tm", 1),), conv_reach)
    residual_ext = stacked_rims[0]
    cotangent_ext = stacked_rims[1][conv_lead : conv_lead + conv_span]
    residual_positions = (
        first_frame - conv_reach + jnp.arange(local_frames + 2 * conv_reach, dtype=jnp.int32)
    )
    residual_seg = segment_ids(starts_row, residual_positions)
    conv_seg = residual_seg[conv_lead : conv_lead + conv_span]
    own_seg = residual_seg[conv_reach : conv_reach + local_frames]
    kernel_float = full_kernel.astype(jnp.float32)
    conv_out = jnp.zeros((conv_span, residual.shape[1]), jnp.float32)
    for offset in range(KW):
        same_utt = (conv_seg == residual_seg[offset : offset + conv_span])[:, None]
        conv_out = conv_out + jnp.where(
            same_utt,
            kernel_float[offset] * residual_ext[offset : offset + conv_span].astype(jnp.float32),
            0.0,
        )
    gate_sig = jax.nn.sigmoid(conv_out)
    gated_grad = cotangent_ext.astype(jnp.float32) * gate_sig * (1.0 + conv_out * (1.0 - gate_sig))
    back_sum = cotangent_rows.astype(jnp.float32)
    own_lower = conv_lead - 1
    own_grad = gated_grad[own_lower : own_lower + local_frames]
    own_conv_seg = conv_seg[own_lower : own_lower + local_frames]
    for offset in range(KW):
        lower = KW - 1 - offset
        same_back = (conv_seg[lower : lower + local_frames] == own_seg)[:, None]
        back_sum = back_sum + jnp.where(
            same_back, kernel_float[offset] * gated_grad[lower : lower + local_frames], 0.0
        )
    products = jnp.stack(
        [
            jnp.where(
                (
                    own_conv_seg
                    == residual_seg[own_lower + offset : own_lower + offset + local_frames]
                )[:, None],
                own_grad
                * residual_ext[own_lower + offset : own_lower + offset + local_frames].astype(
                    jnp.float32
                ),
                0.0,
            )
            for offset in range(KW)
        ]
    )
    kernel_part = jnp.sum(products, axis=1)
    residual_grad = back_sum.astype(jnp.bfloat16)
    context_grad = lax.dot_general(
        residual_grad, full_weight, (((1,), (1,)), ((), ())), preferred_element_type=jnp.float32
    ).astype(jnp.bfloat16)
    grad_scale = 1.0 / math.sqrt(lax.axis_size("fsdp") * queries.shape[0] * frames_total)
    weight_part = (
        lax.dot_general(
            context, residual_grad, (((0,), (0,)), ((), ())), preferred_element_type=jnp.float32
        )
        * grad_scale
    )
    weight_share, kernel_share = (
        lax.psum_scatter(
            weight_part.astype(jnp.bfloat16), "fsdp", scatter_dimension=0, tiled=True
        ).astype(jnp.float32),
        lax.psum_scatter(
            (kernel_part * grad_scale).astype(jnp.bfloat16), "fsdp", scatter_dimension=1, tiled=True
        ).astype(jnp.float32),
    )
    weight_grad, kernel_grad = lax.psum((weight_share, kernel_share), "tm")
    return (context_grad[None], weight_grad, kernel_grad)


MESH = pl.DeviceIdType.MESH
KEY_PAD = 96
ROW_PAD = 32
COT_PAD = 16
GROUP = 32
BLOCK = 64
LANES = 128


def dot(a, b):
    return jnp.dot(a, b, preferred_element_type=jnp.float32)


def dot_t(a, b):
    return lax.dot_general(a, b, (((1,), (1,)), ((), ())), preferred_element_type=jnp.float32)


def block_kernel(
    nt, nf,
    starts_ref, q_ref, kv_ref, in_ref, cot_ref, w_ref, ck_ref,
    cg_ref, wg_ref, kg_ref,
    kvx, qx, inx, cotx, wfull, kall, kf, seg, m1, ctx, ctx_t, res, gs, rg, kgs, kgp, ms,
    part, asrc, abuf, bsrc, bbuf, fsum, csrc, cbuf, gbuf,
    kgsrc, kgb, kgcs, kgc, kgds, kgd,
    ls, hs, hr, ws, wr, fs, fr, ks, kr, as_, ar, bs, br, cs, cr, gsn, grc, ds_, dr,
    kbs, kbr, kcs, kcr, kds, kdr,
):
    nz = nt // 2
    t = lax.axis_index("tm")
    f = lax.axis_index("fsdp")
    z = lax.div(t, 2)
    c = lax.rem(t, 2)
    sib = t + 1 - 2 * c
    rows = q_ref.shape[0]
    shard = w_ref.shape[0]
    half = shard // 2
    width = in_ref.shape[1]
    head_width = q_ref.shape[1]
    head_size = head_width // HEADS_W
    chunks = width // LANES
    per_shard = chunks // nf
    chunk_w = width // nz
    per_piece = chunks // nz
    ext = rows + 2 * ROW_PAD
    span = rows + 2 * COT_PAD
    first = t * rows
    total = nt * rows
    grad_scale = 1.0 / math.sqrt(nf * total)

    def other_f(i):
        return lax.rem(f + i, nf)

    def from_f(i):
        return lax.rem(f + nf - i, nf)

    def other_z(i):
        return lax.rem(z + i, nz)

    def copy(src, dst, send, recv, tm, fsdp):
        return pltpu.make_async_remote_copy(
            src_ref=src, dst_ref=dst, send_sem=send, recv_sem=recv,
            device_id={"tm": tm, "fsdp": fsdp}, device_id_type=MESH,
        )

    halo = ((kv_ref, kvx, KEY_PAD), (q_ref, qx, ROW_PAD), (in_ref, inx, ROW_PAD), (cot_ref, cotx, COT_PAD))
    own_copies = [
        pltpu.make_async_copy(src, dst.at[pl.ds(pad, rows)], ls.at[n])
        for n, (src, dst, pad) in enumerate(halo)
    ]
    own_copies.append(
        pltpu.make_async_copy(
            w_ref, wfull.at[pl.ds(pl.multiple_of(f * shard, 16), shard)], ls.at[4]
        )
    )
    own_copies.append(pltpu.make_async_copy(ck_ref, kall.at[f], ls.at[5]))
    for own_copy in own_copies:
        own_copy.start()

    barrier = pltpu.get_barrier_semaphore()

    def greet(tm, fsdp):
        pl.semaphore_signal(
            barrier, inc=1, device_id={"tm": tm, "fsdp": fsdp}, device_id_type=MESH
        )

    for i in range(1, nf):
        greet(t, other_f(i))
    for i in range(1, nz):
        greet(2 * other_z(i) + c, f)

    @pl.when(t > 0)
    def _():
        greet(t - 1, f)

    @pl.when(t < nt - 1)
    def _():
        greet(t + 1, f)

    near = jnp.minimum(t, 1) + jnp.minimum(nt - 1 - t, 1)
    pl.semaphore_wait(barrier, nf - 1 + nz - 1 + near)

    def up_copy(n):
        src, dst, pad = halo[n]
        return copy(
            src.at[pl.ds(rows - pad, pad)], dst.at[pl.ds(0, pad)], hs.at[0, n], hr.at[0, n], t + 1, f
        )

    def down_copy(n):
        src, dst, pad = halo[n]
        return copy(
            src.at[pl.ds(0, pad)], dst.at[pl.ds(pad + rows, pad)], hs.at[1, n], hr.at[1, n], t - 1, f
        )

    @pl.when(t < nt - 1)
    def _():
        for n in range(4):
            up_copy(n).start()

    @pl.when(t > 0)
    def _():
        for n in range(4):
            down_copy(n).start()

    def rows_of(owner, core):
        return pl.ds(pl.multiple_of(owner * shard + core * half, 16), half)

    def cols(j):
        return pl.ds(chunk_w * j, chunk_w)

    def w_copy(j, i):
        return copy(
            w_ref.at[pl.ds(pl.multiple_of(c * half, 16), half), cols(j)],
            wfull.at[rows_of(f, c), cols(j)], ws.at[j, i], wr.at[j, i], t, other_f(i),
        )

    k_copies = [
        copy(ck_ref, kall.at[f], ks.at[i], kr.at[i], t, other_f(i)) for i in range(1, nf)
    ]
    for k_copy in k_copies:
        k_copy.start()
    for j in range(nz):
        for i in range(1, nf):
            w_copy(j, i).start()

    @pl.when(t == 0)
    def _():
        for src, dst, pad in halo:
            dst[0:pad] = jnp.zeros((pad, dst.shape[1]), dst.dtype)

    @pl.when(t == nt - 1)
    def _():
        for src, dst, pad in halo:
            dst[pad + rows : 2 * pad + rows] = jnp.zeros((pad, dst.shape[1]), dst.dtype)


    utts = starts_ref.shape[1]

    def segments(positions):
        found = jnp.full(positions.shape, -1.0, jnp.float32)
        for u in range(utts):
            found = found + jnp.where(starts_ref[0, u] <= positions, 1.0, 0.0)
        return jnp.where(positions < total, found, -1.0)

    seg[...] = segments(lax.broadcasted_iota(jnp.int32, (ext, LANES), 0) + (first - ROW_PAD))

    for k in range(KW + 1):
        m1[k] = jnp.where(seg[k : k + span] == seg[COT_PAD : COT_PAD + span], 1.0, 0.0)

    def halo_arrived(arrays):
        @pl.when(t > 0)
        def _():
            for n in arrays:
                up_copy(n).wait_recv()

        @pl.when(t < nt - 1)
        def _():
            for n in arrays:
                down_copy(n).wait_recv()

    def forward(j, i):
        piece = wfull.at[rows_of(from_f(i), c), cols(j)]
        return copy(piece, piece, fs.at[j, i], fr.at[j, i], sib, f)

    def pass_on(j):
        for i in range(1, nf):
            w_copy(j, i).wait_recv()
            forward(j, i).start()

    halo_arrived((0, 1))
    for own_copy in own_copies:
        own_copy.wait()
    pass_on(0)

    keys = 2 * LANES
    key_rows = rows + 2 * KEY_PAD
    scale = 1.0 / math.sqrt(head_size)
    lane = lax.broadcasted_iota(jnp.int32, (1, keys), 1)
    for b in range(ext // BLOCK):
        start = min(BLOCK * b, key_rows - keys)
        key_seg = segments(lane + (first - KEY_PAD + start))
        query_seg = seg[BLOCK * b : BLOCK * (b + 1)]
        query_seg = jnp.concatenate([query_seg, query_seg], axis=1)
        gap = (
            lax.broadcasted_iota(jnp.int32, (BLOCK, keys), 1)
            - lax.broadcasted_iota(jnp.int32, (BLOCK, keys), 0)
            + (start - KEY_PAD - BLOCK * b + ROW_PAD)
        )
        allowed = (gap >= -(WIN // 2)) & (gap <= WIN // 2) & (query_seg == key_seg)
        bias = jnp.where(allowed, 0.0, masked_score)
        bias = jnp.concatenate([bias, bias], axis=0)
        for g in range(HEADS_W // 4):
            pairs = []
            for p in range(2):
                base = 4 * head_size * g + LANES * p
                lower = (2 * head_size - LANES) * p
                middle, upper = lower + head_size, lower + 2 * head_size
                in_a = jnp.where((lane >= lower) & (lane < middle), 1.0, 0.0)
                in_b = jnp.where((lane >= middle) & (lane < upper), 1.0, 0.0)
                query = qx[BLOCK * b : BLOCK * (b + 1), base : base + keys]
                query = jnp.concatenate(
                    [query * in_a.astype(jnp.bfloat16), query * in_b.astype(jnp.bfloat16)], axis=0
                )
                scores = dot_t(query, kvx[start : start + keys, base : base + keys]) * scale + bias
                weights = jnp.exp(scores - jnp.max(scores, axis=1, keepdims=True))
                probs = (weights / jnp.sum(weights, axis=1, keepdims=True)).astype(jnp.bfloat16)
                value = dot(
                    probs,
                    kvx[start : start + keys, head_width + base : head_width + base + keys],
                )
                pairs.append(value[:BLOCK] * in_a + value[BLOCK:] * in_b)
            joined = jnp.concatenate(
                [
                    pairs[0][:, :LANES],
                    pairs[0][:, LANES:] + pairs[1][:, :LANES],
                    pairs[1][:, LANES:],
                ],
                axis=1,
            )
            ctx[BLOCK * b : BLOCK * (b + 1), 4 * head_size * g : 4 * head_size * (g + 1)] = (
                joined.astype(jnp.bfloat16)
            )
    ctx_t[...] = ctx[ROW_PAD : ROW_PAD + rows].astype(jnp.float32).T.astype(jnp.bfloat16)

    pass_on(1)
    halo_arrived((2, 3))
    for i in range(1, nf):
        k_copies[i - 1].wait_recv()
    for s in range(nf):
        for i in range(per_shard):
            taps = kall[s, :, LANES * i : LANES * (i + 1)].astype(jnp.float32)
            for k in range(KW):
                kf[s * per_shard + i, k] = jnp.broadcast_to(taps[k : k + 1], (8, LANES))
    def project(j):
        for i in range(1, nf):
            forward(j, i).wait_recv()
        columns = slice(chunk_w * j, chunk_w * (j + 1))
        out = inx[:, columns].astype(jnp.float32) + dot(ctx[...], wfull[:, columns])
        out = out.astype(jnp.bfloat16).astype(jnp.float32)
        for i in range(per_piece):
            res[per_piece * j + i] = out[:, LANES * i : LANES * (i + 1)]

    def tiles(x):
        return x.reshape(x.shape[:-2] + (x.shape[-2] // 8, 8, LANES))

    def conv_group(j):
        lanes = slice(per_piece * j, per_piece * (j + 1))

        def cot_rows(lead):
            return jnp.stack(
                [
                    cotx[lead : lead + GROUP, LANES * n : LANES * (n + 1)].astype(jnp.float32)
                    for n in range(per_piece * j, per_piece * (j + 1))
                ]
            )

        for lead in range(0, span, GROUP):
            conv = jnp.zeros((per_piece, GROUP // 8, 8, LANES), jnp.float32)
            for b in range(8):
                shifted = tiles(res[lanes, lead + b : lead + b + GROUP + 24, :])
                for a in range(KW // 8):
                    k = 8 * a + b
                    mask = tiles(m1[k, lead : lead + GROUP])
                    kept = mask[None] * shifted[:, a : a + GROUP // 8]
                    ms[k, :, lead : lead + GROUP] = kept.reshape(per_piece, GROUP, LANES)
                    conv = conv + kf[lanes, k][:, None] * kept
            conv = conv.reshape(per_piece, GROUP, LANES)
            sig = jax.nn.sigmoid(conv)
            gs[:, lead : lead + GROUP] = cot_rows(lead) * sig * (1.0 + conv * (1.0 - sig))
        if j >= 1:
            finish_a(j - 1)
        for lead in range(0, rows, GROUP):
            mid = slice(COT_PAD + lead, COT_PAD + lead + GROUP)
            back = tiles(cot_rows(COT_PAD + lead))
            for b in range(8):
                low = 8 if b == 0 else 0
                shifted = tiles(gs[:, lead + b + low : lead + b + low + GROUP + 24])
                for a in range(KW // 8):
                    o = 8 * a + b + low
                    mask = tiles(m1[o, mid])
                    back = back + mask[None] * (
                        kf[lanes, KW - o][:, None] * shifted[:, a : a + GROUP // 8]
                    )
            back = back.reshape(per_piece, GROUP, LANES).astype(jnp.bfloat16)
            for i in range(per_piece):
                n = per_piece * j + i
                rg[lead : lead + GROUP, LANES * n : LANES * (n + 1)] = back[i]
        for lead in range(0, rows, 2 * GROUP):
            mid = slice(COT_PAD + lead, COT_PAD + lead + 2 * GROUP)
            grad = tiles(gs[:, mid])
            for k in range(KW):
                prod = jnp.sum(grad * tiles(ms[k, :, mid]), axis=1)
                kgp[k] = prod if lead == 0 else prod + kgp[k]
        for i in range(per_piece):
            kgs[per_piece * j + i] = jnp.sum(kgp[:, i], axis=1)

    def a_copy(j):
        return copy(asrc.at[j], abuf.at[j], as_.at[j], ar.at[j], sib, f)

    def b_copy(j, i):
        return copy(
            bsrc.at[j, other_f(i)], bbuf.at[j, i], bs.at[j, i], br.at[j, i], t, other_f(i)
        )

    owners = sorted(range(nz), key=lambda s: -abs(2 * s - nz + 1))

    def c_copy(j):
        return copy(csrc.at[j], cbuf.at[z], cs.at[j], cr.at[z], 2 * owners[j] + c, f)

    def c_from(i):
        s = other_z(i)
        return copy(csrc.at[0], cbuf.at[s], cs.at[0], cr.at[s], 2 * s + c, f)

    def g_copy(j, i):
        piece = gbuf.at[c, j]
        return copy(piece, piece, gsn.at[i], grc.at[j], 2 * other_z(i) + c, f)

    def d_copy(j):
        piece = gbuf.at[c, j]
        return copy(piece, piece, ds_.at[j], dr.at[j], sib, f)

    def d_from(j):
        piece = gbuf.at[1 - c, j]
        return copy(piece, piece, ds_.at[j], dr.at[j], sib, f)

    def finish_c(j):
        @pl.when(z == owners[j])
        def _():
            final = fsum[...]
            for i in range(1, nz):
                c_from(i).wait_recv()
                final = final + cbuf[other_z(i)].astype(jnp.float32)
            gbuf[c, j] = final.astype(jnp.bfloat16)
            for i in range(1, nz):
                g_copy(j, i).start()
            d_copy(j).start()

    def take(j):
        @pl.when(z != owners[j])
        def _():
            g_copy(j, 1).wait_recv()
            d_copy(j).start()

    def finish_a(j):
        a_copy(j).wait_recv()
        for s in range(nf):
            bsrc[j, s] = (part[j, rows_of(s, c)] + abuf[j, s].astype(jnp.float32)).astype(jnp.bfloat16)
        for i in range(1, nf):
            b_copy(j, i).start()

    def finish_b(j):
        acc = part[j, rows_of(f, c)] + abuf[j, f].astype(jnp.float32)
        for i in range(1, nf):
            b_copy(j, i).wait_recv()
            acc = acc + bbuf[j, i].astype(jnp.float32)

        @pl.when(z == owners[j])
        def _():
            fsum[...] = acc

        @pl.when(z != owners[j])
        def _():
            csrc[j] = acc.astype(jnp.bfloat16)
            c_copy(j).start()

    for j in range(nz):
        project(j)
        if j + 2 < nz:
            pass_on(j + 2)
        conv_group(j)
        part[j] = dot(ctx_t[...], rg[:, chunk_w * j : chunk_w * (j + 1)])
        for s in range(nf):
            asrc[j, s] = part[j, rows_of(s, 1 - c)].astype(jnp.bfloat16)
        a_copy(j).start()
        if j >= 2:
            finish_b(j - 2)
        if j >= 3:
            finish_c(j - 3)

    def kb_copy(i):
        return copy(kgsrc.at[other_f(i)], kgb.at[i], kbs.at[i], kbr.at[i], t, other_f(i))

    for s in range(nf):
        for i in range(per_shard):
            kgsrc[s, i] = kgs[s * per_shard + i].astype(jnp.bfloat16)
    for i in range(1, nf):
        kb_copy(i).start()
    finish_a(nz - 1)
    if nz >= 2:
        finish_b(nz - 2)
    if nz >= 3:
        finish_c(nz - 3)
    cg_ref[...] = dot_t(rg[...], wfull[...]).astype(jnp.bfloat16)

    kg_sum = kgs[pl.ds(f * per_shard, per_shard)]
    for i in range(1, nf):
        kb_copy(i).wait_recv()
        kg_sum = kg_sum + kgb[i].astype(jnp.float32)
    kgcs[...] = kg_sum.astype(jnp.bfloat16)

    def kc_copy(i):
        return copy(kgcs, kgc.at[z], kcs.at[i], kcr.at[z], 2 * other_z(i) + c, f)

    def kc_from(i):
        s = other_z(i)
        return copy(kgcs, kgc.at[s], kcs.at[i], kcr.at[s], 2 * s + c, f)

    for i in range(1, nz):
        kc_copy(i).start()
    kgc[z] = kgcs[...]
    finish_b(nz - 1)

    if nz >= 2:
        finish_c(nz - 2)
    for j in range(nz - 2):
        take(j)
    finish_c(nz - 1)

    for i in range(1, nz):
        kc_from(i).wait_recv()
    kg_z = kgc[0].astype(jnp.float32)
    for s in range(1, nz):
        kg_z = kg_z + kgc[s].astype(jnp.float32)
    kgds[...] = kg_z.astype(jnp.bfloat16)
    kd_copy = copy(kgds, kgd, kds, kdr, sib, f)
    kd_copy.start()

    for j in range(max(nz - 2, 0), nz):
        take(j)
    kd_copy.wait_recv()
    kg_all = kgds[...].astype(jnp.float32) + kgd[...].astype(jnp.float32)
    for i in range(per_shard):
        kg_ref[:, LANES * i : LANES * (i + 1)] = kg_all[i] * grad_scale
    mine = pl.ds(pl.multiple_of(c * half, 16), half)
    theirs = pl.ds(pl.multiple_of((1 - c) * half, 16), half)
    for s in range(nz):
        wg_ref[mine, chunk_w * s : chunk_w * (s + 1)] = gbuf[c, s].astype(jnp.float32) * grad_scale
    for s in range(nz):
        d_from(s).wait_recv()
        wg_ref[theirs, chunk_w * s : chunk_w * (s + 1)] = gbuf[1 - c, s].astype(jnp.float32) * grad_scale

    @pl.when(t < nt - 1)
    def _():
        for n in range(4):
            up_copy(n).wait_send()

    @pl.when(t > 0)
    def _():
        for n in range(4):
            down_copy(n).wait_send()

    for i in range(1, nf):
        k_copies[i - 1].wait_send()
        kb_copy(i).wait_send()
    for j in range(nz):
        a_copy(j).wait_send()
        for i in range(1, nf):
            w_copy(j, i).wait_send()
            forward(j, i).wait_send()
            b_copy(j, i).wait_send()

        @pl.when(z != owners[j])
        def _():
            c_copy(j).wait_send()

    for i in range(1, nz):
        kc_copy(i).wait_send()
        g_copy(0, i).wait_send()
    for j in range(nz):
        d_copy(j).wait_send()
    kd_copy.wait_send()


def fused(nt, nf, queries, keys_values, inputs, cotangent, out_weight, conv_kernel, utt_starts):
    rows, head_width = queries.shape[1:]
    width = inputs.shape[2]
    nz = nt // 2
    shard = out_weight.shape[0]
    half = shard // 2
    chunks = width // LANES
    per_shard = chunks // nf
    chunk_w = width // nz
    per_piece = chunks // nz
    ext = rows + 2 * ROW_PAD
    span = rows + 2 * COT_PAD
    bf16, f32 = jnp.bfloat16, jnp.float32
    dma = pltpu.SemaphoreType.DMA
    vmem = pl.BlockSpec(memory_space=pltpu.VMEM)
    scratch = [
        ((rows + 2 * KEY_PAD, 2 * head_width), bf16),
        ((ext, head_width), bf16),
        ((ext, width), bf16),
        ((span, width), bf16),
        ((head_width, width), bf16),
        ((nf, KW, width // nf), bf16),
        ((chunks, KW, 8, LANES), f32),
        ((ext, LANES), f32),
        ((KW + 1, span, LANES), f32),
        ((ext, head_width), bf16),
        ((head_width, rows), bf16),
        ((chunks, ext, LANES), f32),
        ((per_piece, span, LANES), f32),
        ((rows, width), bf16),
        ((chunks, KW, LANES), f32),
        ((KW, per_piece, 8, LANES), f32),
        ((KW, per_piece, span, LANES), f32),
        ((nz, head_width, chunk_w), f32),
        ((nz, nf, half, chunk_w), bf16),
        ((nz, nf, half, chunk_w), bf16),
        ((nz, nf, half, chunk_w), bf16),
        ((nz, nf, half, chunk_w), bf16),
        ((half, chunk_w), f32),
        ((nz, half, chunk_w), bf16),
        ((nz, half, chunk_w), bf16),
        ((2, nz, half, chunk_w), bf16),
        ((nf, per_shard, KW, LANES), bf16),
        ((nf, per_shard, KW, LANES), bf16),
        ((per_shard, KW, LANES), bf16),
        ((nz, per_shard, KW, LANES), bf16),
        ((per_shard, KW, LANES), bf16),
        ((per_shard, KW, LANES), bf16),
    ]
    sems = [
        (6,), (2, 4), (2, 4), (nz, nf), (nz, nf), (nz, nf), (nz, nf), (nf,), (nf,), (nz,), (nz,), (nz, nf), (nz, nf),
        (nz,), (nz,), (nz,), (nz,), (nz,), (nz,), (nf,), (nf,), (nz,), (nz,),
    ]
    context_grad, weight_grad, kernel_grad = pl.pallas_call(
        functools.partial(block_kernel, nt, nf),
        out_shape=(
            jax.ShapeDtypeStruct((rows, head_width), bf16),
            jax.ShapeDtypeStruct((shard, width), f32),
            jax.ShapeDtypeStruct((KW, width // nf), f32),
        ),
        in_specs=[pl.BlockSpec(memory_space=pltpu.SMEM)] + [pl.BlockSpec(memory_space=pltpu.HBM)] * 6,
        out_specs=(vmem, vmem, vmem),
        scratch_shapes=[pltpu.VMEM(*s) for s in scratch]
        + [dma(s) for s in sems]
        + [dma, dma],
        compiler_params=pltpu.CompilerParams(
            collective_id=0, has_side_effects=True, vmem_limit_bytes=60 * 1024 * 1024
        ),
    )(utt_starts, queries[0], keys_values[0], inputs[0], cotangent[0], out_weight, conv_kernel)
    return (context_grad[None], weight_grad, kernel_grad)


def fits(nt, nf, queries, keys_values, inputs, cotangent, out_weight, conv_kernel, utt_starts):
    rows, head_width = queries.shape[1:]
    width = inputs.shape[2]
    return (
        queries.shape[0] == 1
        and rows == 2 * BLOCK
        and nt % 2 == 0
        and nt >= 4
        and (width // LANES) % (nt // 2) == 0
        and (width // LANES) % nf == 0
        and out_weight.shape[0] % 32 == 0
        and head_width * LANES == HEADS_W * 96 * LANES
    )


def solution(mesh):
    nt, nf = mesh.shape["tm"], mesh.shape["fsdp"]

    def body(*arrays):
        if fits(nt, nf, *arrays):
            return fused(nt, nf, *arrays)
        return shards(*arrays)

    return jax.shard_map(
        body,
        mesh=mesh,
        in_specs=(
            P("fsdp", "tm", None),
            P("fsdp", "tm", None),
            P("fsdp", "tm", None),
            P("fsdp", "tm", None),
            P("fsdp", None),
            P(None, "fsdp"),
            P("fsdp", None),
        ),
        out_specs=(P("fsdp", "tm", None), P("fsdp", None), P(None, "fsdp")),
        check_vma=False,
    )
```

```python
import functools
import math

import jax
import jax.numpy as jnp
from jax import lax
from jax.experimental import pallas as pl
from jax.experimental.pallas import tpu as pltpu
from jax.sharding import PartitionSpec as P

HEADS_W = 8
KW = 32
WIN = 128


masked_score = -1e30


def with_halo(x, sides, width):
    for axis, dim in sides:
        devices, length = (lax.axis_size(axis), x.shape[dim])
        up = [(i, (i + 1) % devices) for i in range(devices - 1)]
        down = [(j, i) for i, j in up]
        last = lax.slice_in_dim(x, length - width, length, axis=dim)
        initial = lax.slice_in_dim(x, 0, width, axis=dim)
        before = lax.ppermute(last, axis, up)
        after = lax.ppermute(initial, axis, down)
        x = jnp.concatenate([before, x, after], axis=dim)
    return x


def segment_ids(starts_row, positions):
    return jnp.sum((starts_row[None, :] <= positions[:, None]).astype(jnp.int32), axis=1) - 1


def shards(queries, keys_values, inputs, cotangent, out_weight, conv_kernel, utt_starts):
    query_rows = queries[0]
    kv_rows = keys_values[0]
    input_rows = inputs[0]
    cotangent_rows = cotangent[0]
    starts_row = utt_starts[0]
    local_frames = query_rows.shape[0]
    head_width = query_rows.shape[1]
    head_size = head_width // HEADS_W
    window_half = WIN // 2
    conv_reach = KW - 1
    conv_lead = KW // 2
    conv_span = local_frames + KW - 1
    frames_total = local_frames * lax.axis_size("tm")
    first_frame = lax.axis_index("tm") * local_frames
    full_weight, full_kernel = (
        lax.all_gather(out_weight, "fsdp", axis=0, tiled=True),
        lax.all_gather(conv_kernel, "fsdp", axis=1, tiled=True),
    )
    kv_ext = with_halo(kv_rows, (("tm", 0),), window_half)
    key_span = local_frames + 2 * window_half
    key_positions = first_frame - window_half + jnp.arange(key_span, dtype=jnp.int32)
    key_seg = jnp.where(key_positions < frames_total, segment_ids(starts_row, key_positions), -1)
    query_seg = segment_ids(starts_row, first_frame + jnp.arange(local_frames, dtype=jnp.int32))
    key_offset = (
        jnp.arange(key_span, dtype=jnp.int32)[None, :]
        - jnp.arange(local_frames, dtype=jnp.int32)[:, None]
    )
    allowed = (
        (key_offset >= 0)
        & (key_offset <= 2 * window_half)
        & (query_seg[:, None] == key_seg[None, :])
    )
    query_heads = query_rows.reshape(local_frames, HEADS_W, head_size)
    key_heads = kv_ext[:, :head_width].reshape(key_span, HEADS_W, head_size)
    value_heads = kv_ext[:, head_width:].reshape(key_span, HEADS_W, head_size)
    scores = jnp.einsum(
        "qhe,khe->hqk", query_heads, key_heads, preferred_element_type=jnp.float32
    ) / math.sqrt(head_size)
    scores = jnp.where(allowed[None], scores, masked_score)
    row_max = jnp.max(scores, axis=2, keepdims=True)
    exp_scores = jnp.exp(scores - row_max)
    attn_probs = (exp_scores / jnp.sum(exp_scores, axis=2, keepdims=True)).astype(jnp.bfloat16)
    context = jnp.einsum(
        "hqk,khe->qhe", attn_probs, value_heads, preferred_element_type=jnp.float32
    )
    context = context.reshape(local_frames, head_width).astype(jnp.bfloat16)
    residual = (
        input_rows.astype(jnp.float32)
        + jnp.dot(context, full_weight, preferred_element_type=jnp.float32)
    ).astype(jnp.bfloat16)
    stacked_rims = with_halo(jnp.stack([residual, cotangent_rows]), (("tm", 1),), conv_reach)
    residual_ext = stacked_rims[0]
    cotangent_ext = stacked_rims[1][conv_lead : conv_lead + conv_span]
    residual_positions = (
        first_frame - conv_reach + jnp.arange(local_frames + 2 * conv_reach, dtype=jnp.int32)
    )
    residual_seg = segment_ids(starts_row, residual_positions)
    conv_seg = residual_seg[conv_lead : conv_lead + conv_span]
    own_seg = residual_seg[conv_reach : conv_reach + local_frames]
    kernel_float = full_kernel.astype(jnp.float32)
    conv_out = jnp.zeros((conv_span, residual.shape[1]), jnp.float32)
    for offset in range(KW):
        same_utt = (conv_seg == residual_seg[offset : offset + conv_span])[:, None]
        conv_out = conv_out + jnp.where(
            same_utt,
            kernel_float[offset] * residual_ext[offset : offset + conv_span].astype(jnp.float32),
            0.0,
        )
    gate_sig = jax.nn.sigmoid(conv_out)
    gated_grad = cotangent_ext.astype(jnp.float32) * gate_sig * (1.0 + conv_out * (1.0 - gate_sig))
    back_sum = cotangent_rows.astype(jnp.float32)
    own_lower = conv_lead - 1
    own_grad = gated_grad[own_lower : own_lower + local_frames]
    own_conv_seg = conv_seg[own_lower : own_lower + local_frames]
    for offset in range(KW):
        lower = KW - 1 - offset
        same_back = (conv_seg[lower : lower + local_frames] == own_seg)[:, None]
        back_sum = back_sum + jnp.where(
            same_back, kernel_float[offset] * gated_grad[lower : lower + local_frames], 0.0
        )
    products = jnp.stack(
        [
            jnp.where(
                (
                    own_conv_seg
                    == residual_seg[own_lower + offset : own_lower + offset + local_frames]
                )[:, None],
                own_grad
                * residual_ext[own_lower + offset : own_lower + offset + local_frames].astype(
                    jnp.float32
                ),
                0.0,
            )
            for offset in range(KW)
        ]
    )
    kernel_part = jnp.sum(products, axis=1)
    residual_grad = back_sum.astype(jnp.bfloat16)
    context_grad = lax.dot_general(
        residual_grad, full_weight, (((1,), (1,)), ((), ())), preferred_element_type=jnp.float32
    ).astype(jnp.bfloat16)
    grad_scale = 1.0 / math.sqrt(lax.axis_size("fsdp") * queries.shape[0] * frames_total)
    weight_part = (
        lax.dot_general(
            context, residual_grad, (((0,), (0,)), ((), ())), preferred_element_type=jnp.float32
        )
        * grad_scale
    )
    weight_share, kernel_share = (
        lax.psum_scatter(
            weight_part.astype(jnp.bfloat16), "fsdp", scatter_dimension=0, tiled=True
        ).astype(jnp.float32),
        lax.psum_scatter(
            (kernel_part * grad_scale).astype(jnp.bfloat16), "fsdp", scatter_dimension=1, tiled=True
        ).astype(jnp.float32),
    )
    weight_grad, kernel_grad = lax.psum((weight_share, kernel_share), "tm")
    return (context_grad[None], weight_grad, kernel_grad)


MESH = pl.DeviceIdType.MESH
KEY_PAD = 96
ROW_PAD = 32
COT_PAD = 16
GROUP = 32
BLOCK = 64
LANES = 128


def dot(a, b):
    return jnp.dot(a, b, preferred_element_type=jnp.float32)


def dot_t(a, b):
    return lax.dot_general(a, b, (((1,), (1,)), ((), ())), preferred_element_type=jnp.float32)


def block_kernel(
    nt, nf,
    starts_ref, q_ref, kv_ref, in_ref, cot_ref, w_ref, ck_ref,
    cg_ref, wg_ref, kg_ref,
    kvx, qx, inx, cotx, wfull, kall, kf, seg, m1, ctx, ctx_t, res, gs, rg, kgs, kgp, ms,
    part, asrc, abuf, bsrc, bbuf, fsum, csrc, cbuf, gbuf,
    kgsrc, kgb, kgcs, kgc, kgds, kgd,
    ls, hs, hr, ws, wr, fs, fr, ks, kr, as_, ar, bs, br, cs, cr, gsn, grc, ds_, dr,
    kbs, kbr, kcs, kcr, kds, kdr,
):
    nz = nt // 2
    t = lax.axis_index("tm")
    f = lax.axis_index("fsdp")
    z = lax.div(t, 2)
    c = lax.rem(t, 2)
    sib = t + 1 - 2 * c
    rows = q_ref.shape[0]
    shard = w_ref.shape[0]
    half = shard // 2
    width = in_ref.shape[1]
    head_width = q_ref.shape[1]
    head_size = head_width // HEADS_W
    chunks = width // LANES
    per_shard = chunks // nf
    chunk_w = width // nz
    per_piece = chunks // nz
    ext = rows + 2 * ROW_PAD
    span = rows + 2 * COT_PAD
    first = t * rows
    total = nt * rows
    grad_scale = 1.0 / math.sqrt(nf * total)

    def other_f(i):
        return lax.rem(f + i, nf)

    def from_f(i):
        return lax.rem(f + nf - i, nf)

    def other_z(i):
        return lax.rem(z + i, nz)

    def copy(src, dst, send, recv, tm, fsdp):
        return pltpu.make_async_remote_copy(
            src_ref=src, dst_ref=dst, send_sem=send, recv_sem=recv,
            device_id={"tm": tm, "fsdp": fsdp}, device_id_type=MESH,
        )

    halo = ((kv_ref, kvx, KEY_PAD), (q_ref, qx, ROW_PAD), (in_ref, inx, ROW_PAD), (cot_ref, cotx, COT_PAD))
    own_copies = [
        pltpu.make_async_copy(src, dst.at[pl.ds(pad, rows)], ls.at[n])
        for n, (src, dst, pad) in enumerate(halo)
    ]
    own_copies.append(
        pltpu.make_async_copy(
            w_ref, wfull.at[pl.ds(pl.multiple_of(f * shard, 16), shard)], ls.at[4]
        )
    )
    own_copies.append(pltpu.make_async_copy(ck_ref, kall.at[f], ls.at[5]))
    for own_copy in own_copies:
        own_copy.start()

    barrier = pltpu.get_barrier_semaphore()

    def greet(tm, fsdp):
        pl.semaphore_signal(
            barrier, inc=1, device_id={"tm": tm, "fsdp": fsdp}, device_id_type=MESH
        )

    for i in range(1, nf):
        greet(t, other_f(i))
    for i in range(1, nz):
        greet(2 * other_z(i) + c, f)

    @pl.when(t > 0)
    def _():
        greet(t - 1, f)

    @pl.when(t < nt - 1)
    def _():
        greet(t + 1, f)

    near = jnp.minimum(t, 1) + jnp.minimum(nt - 1 - t, 1)
    pl.semaphore_wait(barrier, nf - 1 + nz - 1 + near)

    def up_copy(n):
        src, dst, pad = halo[n]
        return copy(
            src.at[pl.ds(rows - pad, pad)], dst.at[pl.ds(0, pad)], hs.at[0, n], hr.at[0, n], t + 1, f
        )

    def down_copy(n):
        src, dst, pad = halo[n]
        return copy(
            src.at[pl.ds(0, pad)], dst.at[pl.ds(pad + rows, pad)], hs.at[1, n], hr.at[1, n], t - 1, f
        )

    @pl.when(t < nt - 1)
    def _():
        for n in range(4):
            up_copy(n).start()

    @pl.when(t > 0)
    def _():
        for n in range(4):
            down_copy(n).start()

    def rows_of(owner, core):
        return pl.ds(pl.multiple_of(owner * shard + core * half, 16), half)

    def cols(j):
        return pl.ds(chunk_w * j, chunk_w)

    def w_copy(j, i):
        return copy(
            w_ref.at[pl.ds(pl.multiple_of(c * half, 16), half), cols(j)],
            wfull.at[rows_of(f, c), cols(j)], ws.at[j, i], wr.at[j, i], t, other_f(i),
        )

    k_copies = [
        copy(ck_ref, kall.at[f], ks.at[i], kr.at[i], t, other_f(i)) for i in range(1, nf)
    ]
    for k_copy in k_copies:
        k_copy.start()
    for j in range(nz):
        for i in range(1, nf):
            w_copy(j, i).start()

    @pl.when(t == 0)
    def _():
        for src, dst, pad in halo:
            dst[0:pad] = jnp.zeros((pad, dst.shape[1]), dst.dtype)

    @pl.when(t == nt - 1)
    def _():
        for src, dst, pad in halo:
            dst[pad + rows : 2 * pad + rows] = jnp.zeros((pad, dst.shape[1]), dst.dtype)


    utts = starts_ref.shape[1]

    def segments(positions):
        found = jnp.full(positions.shape, -1.0, jnp.float32)
        for u in range(utts):
            found = found + jnp.where(starts_ref[0, u] <= positions, 1.0, 0.0)
        return jnp.where(positions < total, found, -1.0)

    seg[...] = segments(lax.broadcasted_iota(jnp.int32, (ext, LANES), 0) + (first - ROW_PAD))

    for k in range(KW + 1):
        m1[k] = jnp.where(seg[k : k + span] == seg[COT_PAD : COT_PAD + span], 1.0, 0.0)

    def halo_arrived(arrays):
        @pl.when(t > 0)
        def _():
            for n in arrays:
                up_copy(n).wait_recv()

        @pl.when(t < nt - 1)
        def _():
            for n in arrays:
                down_copy(n).wait_recv()

    def forward(j, i):
        piece = wfull.at[rows_of(from_f(i), c), cols(j)]
        return copy(piece, piece, fs.at[j, i], fr.at[j, i], sib, f)

    def pass_on(j):
        for i in range(1, nf):
            w_copy(j, i).wait_recv()
            forward(j, i).start()

    halo_arrived((0, 1))
    for own_copy in own_copies:
        own_copy.wait()
    pass_on(0)

    keys = 2 * LANES
    key_rows = rows + 2 * KEY_PAD
    scale = 1.0 / math.sqrt(head_size)
    lane = lax.broadcasted_iota(jnp.int32, (1, keys), 1)
    for b in range(ext // BLOCK):
        start = min(BLOCK * b, key_rows - keys)
        key_seg = segments(lane + (first - KEY_PAD + start))
        query_seg = seg[BLOCK * b : BLOCK * (b + 1)]
        query_seg = jnp.concatenate([query_seg, query_seg], axis=1)
        gap = (
            lax.broadcasted_iota(jnp.int32, (BLOCK, keys), 1)
            - lax.broadcasted_iota(jnp.int32, (BLOCK, keys), 0)
            + (start - KEY_PAD - BLOCK * b + ROW_PAD)
        )
        allowed = (gap >= -(WIN // 2)) & (gap <= WIN // 2) & (query_seg == key_seg)
        bias = jnp.where(allowed, 0.0, masked_score)
        bias = jnp.concatenate([bias, bias], axis=0)
        for g in range(HEADS_W // 4):
            pairs = []
            for p in range(2):
                base = 4 * head_size * g + LANES * p
                lower = (2 * head_size - LANES) * p
                middle, upper = lower + head_size, lower + 2 * head_size
                in_a = jnp.where((lane >= lower) & (lane < middle), 1.0, 0.0)
                in_b = jnp.where((lane >= middle) & (lane < upper), 1.0, 0.0)
                query = qx[BLOCK * b : BLOCK * (b + 1), base : base + keys]
                query = jnp.concatenate(
                    [query * in_a.astype(jnp.bfloat16), query * in_b.astype(jnp.bfloat16)], axis=0
                )
                scores = dot_t(query, kvx[start : start + keys, base : base + keys]) * scale + bias
                weights = jnp.exp(scores - jnp.max(scores, axis=1, keepdims=True))
                probs = (weights / jnp.sum(weights, axis=1, keepdims=True)).astype(jnp.bfloat16)
                value = dot(
                    probs,
                    kvx[start : start + keys, head_width + base : head_width + base + keys],
                )
                pairs.append(value[:BLOCK] * in_a + value[BLOCK:] * in_b)
            joined = jnp.concatenate(
                [
                    pairs[0][:, :LANES],
                    pairs[0][:, LANES:] + pairs[1][:, :LANES],
                    pairs[1][:, LANES:],
                ],
                axis=1,
            )
            ctx[BLOCK * b : BLOCK * (b + 1), 4 * head_size * g : 4 * head_size * (g + 1)] = (
                joined.astype(jnp.bfloat16)
            )
    ctx_t[...] = ctx[ROW_PAD : ROW_PAD + rows].astype(jnp.float32).T.astype(jnp.bfloat16)

    pass_on(1)
    halo_arrived((2, 3))
    for i in range(1, nf):
        k_copies[i - 1].wait_recv()
    for s in range(nf):
        for i in range(per_shard):
            taps = kall[s, :, LANES * i : LANES * (i + 1)].astype(jnp.float32)
            for k in range(KW):
                kf[s * per_shard + i, k] = jnp.broadcast_to(taps[k : k + 1], (8, LANES))
    def project(j):
        for i in range(1, nf):
            forward(j, i).wait_recv()
        columns = slice(chunk_w * j, chunk_w * (j + 1))
        out = inx[:, columns].astype(jnp.float32) + dot(ctx[...], wfull[:, columns])
        out = out.astype(jnp.bfloat16).astype(jnp.float32)
        for i in range(per_piece):
            res[per_piece * j + i] = out[:, LANES * i : LANES * (i + 1)]

    def tiles(x):
        return x.reshape(x.shape[:-2] + (x.shape[-2] // 8, 8, LANES))

    def conv_group(j):
        lanes = slice(per_piece * j, per_piece * (j + 1))

        def cot_rows(lead):
            return jnp.stack(
                [
                    cotx[lead : lead + GROUP, LANES * n : LANES * (n + 1)].astype(jnp.float32)
                    for n in range(per_piece * j, per_piece * (j + 1))
                ]
            )

        for lead in range(0, span, GROUP):
            conv = jnp.zeros((per_piece, GROUP // 8, 8, LANES), jnp.float32)
            for b in range(8):
                shifted = tiles(res[lanes, lead + b : lead + b + GROUP + 24, :])
                for a in range(KW // 8):
                    k = 8 * a + b
                    mask = tiles(m1[k, lead : lead + GROUP])
                    kept = mask[None] * shifted[:, a : a + GROUP // 8]
                    ms[k, :, lead : lead + GROUP] = kept.reshape(per_piece, GROUP, LANES)
                    conv = conv + kf[lanes, k][:, None] * kept
            conv = conv.reshape(per_piece, GROUP, LANES)
            sig = jax.nn.sigmoid(conv)
            gs[:, lead : lead + GROUP] = cot_rows(lead) * sig * (1.0 + conv * (1.0 - sig))
        if j >= 1:
            finish_a(j - 1)
        if j >= 2:
            finish_b(j - 2)
        if j >= 3:
            finish_c(j - 3)
        for lead in range(0, rows, GROUP):
            mid = slice(COT_PAD + lead, COT_PAD + lead + GROUP)
            back = tiles(cot_rows(COT_PAD + lead))
            for b in range(8):
                low = 8 if b == 0 else 0
                shifted = tiles(gs[:, lead + b + low : lead + b + low + GROUP + 24])
                for a in range(KW // 8):
                    o = 8 * a + b + low
                    mask = tiles(m1[o, mid])
                    back = back + mask[None] * (
                        kf[lanes, KW - o][:, None] * shifted[:, a : a + GROUP // 8]
                    )
            back = back.reshape(per_piece, GROUP, LANES).astype(jnp.bfloat16)
            for i in range(per_piece):
                n = per_piece * j + i
                rg[lead : lead + GROUP, LANES * n : LANES * (n + 1)] = back[i]
        for lead in range(0, rows, 2 * GROUP):
            mid = slice(COT_PAD + lead, COT_PAD + lead + 2 * GROUP)
            grad = tiles(gs[:, mid])
            for k in range(KW):
                prod = jnp.sum(grad * tiles(ms[k, :, mid]), axis=1)
                kgp[k] = prod if lead == 0 else prod + kgp[k]
        for i in range(per_piece):
            kgs[per_piece * j + i] = jnp.sum(kgp[:, i], axis=1)

    def a_copy(j):
        return copy(asrc.at[j], abuf.at[j], as_.at[j], ar.at[j], sib, f)

    def b_copy(j, i):
        return copy(
            bsrc.at[j, other_f(i)], bbuf.at[j, i], bs.at[j, i], br.at[j, i], t, other_f(i)
        )

    owners = sorted(range(nz), key=lambda s: -abs(2 * s - nz + 1))

    def c_copy(j):
        return copy(csrc.at[j], cbuf.at[z], cs.at[j], cr.at[z], 2 * owners[j] + c, f)

    def c_from(i):
        s = other_z(i)
        return copy(csrc.at[0], cbuf.at[s], cs.at[0], cr.at[s], 2 * s + c, f)

    def g_copy(j, i):
        piece = gbuf.at[c, j]
        return copy(piece, piece, gsn.at[i], grc.at[j], 2 * other_z(i) + c, f)

    def d_copy(j):
        piece = gbuf.at[c, j]
        return copy(piece, piece, ds_.at[j], dr.at[j], sib, f)

    def d_from(j):
        piece = gbuf.at[1 - c, j]
        return copy(piece, piece, ds_.at[j], dr.at[j], sib, f)

    def finish_c(j):
        @pl.when(z == owners[j])
        def _():
            final = fsum[...]
            for i in range(1, nz):
                c_from(i).wait_recv()
                final = final + cbuf[other_z(i)].astype(jnp.float32)
            gbuf[c, j] = final.astype(jnp.bfloat16)
            for i in range(1, nz):
                g_copy(j, i).start()
            d_copy(j).start()

    def take(j):
        @pl.when(z != owners[j])
        def _():
            g_copy(j, 1).wait_recv()
            d_copy(j).start()

    def finish_a(j):
        a_copy(j).wait_recv()
        for s in range(nf):
            bsrc[j, s] = (part[j, rows_of(s, c)] + abuf[j, s].astype(jnp.float32)).astype(jnp.bfloat16)
        for i in range(1, nf):
            b_copy(j, i).start()

    def finish_b(j):
        acc = part[j, rows_of(f, c)] + abuf[j, f].astype(jnp.float32)
        for i in range(1, nf):
            b_copy(j, i).wait_recv()
            acc = acc + bbuf[j, i].astype(jnp.float32)

        @pl.when(z == owners[j])
        def _():
            fsum[...] = acc

        @pl.when(z != owners[j])
        def _():
            csrc[j] = acc.astype(jnp.bfloat16)
            c_copy(j).start()

    for j in range(nz):
        project(j)
        if j + 2 < nz:
            pass_on(j + 2)
        conv_group(j)
        part[j] = dot(ctx_t[...], rg[:, chunk_w * j : chunk_w * (j + 1)])
        for s in range(nf):
            asrc[j, s] = part[j, rows_of(s, 1 - c)].astype(jnp.bfloat16)
        a_copy(j).start()

    def kb_copy(i):
        return copy(kgsrc.at[other_f(i)], kgb.at[i], kbs.at[i], kbr.at[i], t, other_f(i))

    for s in range(nf):
        for i in range(per_shard):
            kgsrc[s, i] = kgs[s * per_shard + i].astype(jnp.bfloat16)
    for i in range(1, nf):
        kb_copy(i).start()
    finish_a(nz - 1)
    if nz >= 2:
        finish_b(nz - 2)
    if nz >= 3:
        finish_c(nz - 3)
    cg_ref[...] = dot_t(rg[...], wfull[...]).astype(jnp.bfloat16)

    kg_sum = kgs[pl.ds(f * per_shard, per_shard)]
    for i in range(1, nf):
        kb_copy(i).wait_recv()
        kg_sum = kg_sum + kgb[i].astype(jnp.float32)
    kgcs[...] = kg_sum.astype(jnp.bfloat16)

    def kc_copy(i):
        return copy(kgcs, kgc.at[z], kcs.at[i], kcr.at[z], 2 * other_z(i) + c, f)

    def kc_from(i):
        s = other_z(i)
        return copy(kgcs, kgc.at[s], kcs.at[i], kcr.at[s], 2 * s + c, f)

    for i in range(1, nz):
        kc_copy(i).start()
    kgc[z] = kgcs[...]
    finish_b(nz - 1)

    if nz >= 2:
        finish_c(nz - 2)
    for j in range(nz - 2):
        take(j)
    finish_c(nz - 1)

    for i in range(1, nz):
        kc_from(i).wait_recv()
    kg_z = kgc[0].astype(jnp.float32)
    for s in range(1, nz):
        kg_z = kg_z + kgc[s].astype(jnp.float32)
    kgds[...] = kg_z.astype(jnp.bfloat16)
    kd_copy = copy(kgds, kgd, kds, kdr, sib, f)
    kd_copy.start()

    for j in range(max(nz - 2, 0), nz):
        take(j)
    kd_copy.wait_recv()
    kg_all = kgds[...].astype(jnp.float32) + kgd[...].astype(jnp.float32)
    for i in range(per_shard):
        kg_ref[:, LANES * i : LANES * (i + 1)] = kg_all[i] * grad_scale
    mine = pl.ds(pl.multiple_of(c * half, 16), half)
    theirs = pl.ds(pl.multiple_of((1 - c) * half, 16), half)
    for s in range(nz):
        wg_ref[mine, chunk_w * s : chunk_w * (s + 1)] = gbuf[c, s].astype(jnp.float32) * grad_scale
    for s in range(nz):
        d_from(s).wait_recv()
        wg_ref[theirs, chunk_w * s : chunk_w * (s + 1)] = gbuf[1 - c, s].astype(jnp.float32) * grad_scale

    @pl.when(t < nt - 1)
    def _():
        for n in range(4):
            up_copy(n).wait_send()

    @pl.when(t > 0)
    def _():
        for n in range(4):
            down_copy(n).wait_send()

    for i in range(1, nf):
        k_copies[i - 1].wait_send()
        kb_copy(i).wait_send()
    for j in range(nz):
        a_copy(j).wait_send()
        for i in range(1, nf):
            w_copy(j, i).wait_send()
            forward(j, i).wait_send()
            b_copy(j, i).wait_send()

        @pl.when(z != owners[j])
        def _():
            c_copy(j).wait_send()

    for i in range(1, nz):
        kc_copy(i).wait_send()
        g_copy(0, i).wait_send()
    for j in range(nz):
        d_copy(j).wait_send()
    kd_copy.wait_send()


def fused(nt, nf, queries, keys_values, inputs, cotangent, out_weight, conv_kernel, utt_starts):
    rows, head_width = queries.shape[1:]
    width = inputs.shape[2]
    nz = nt // 2
    shard = out_weight.shape[0]
    half = shard // 2
    chunks = width // LANES
    per_shard = chunks // nf
    chunk_w = width // nz
    per_piece = chunks // nz
    ext = rows + 2 * ROW_PAD
    span = rows + 2 * COT_PAD
    bf16, f32 = jnp.bfloat16, jnp.float32
    dma = pltpu.SemaphoreType.DMA
    vmem = pl.BlockSpec(memory_space=pltpu.VMEM)
    scratch = [
        ((rows + 2 * KEY_PAD, 2 * head_width), bf16),
        ((ext, head_width), bf16),
        ((ext, width), bf16),
        ((span, width), bf16),
        ((head_width, width), bf16),
        ((nf, KW, width // nf), bf16),
        ((chunks, KW, 8, LANES), f32),
        ((ext, LANES), f32),
        ((KW + 1, span, LANES), f32),
        ((ext, head_width), bf16),
        ((head_width, rows), bf16),
        ((chunks, ext, LANES), f32),
        ((per_piece, span, LANES), f32),
        ((rows, width), bf16),
        ((chunks, KW, LANES), f32),
        ((KW, per_piece, 8, LANES), f32),
        ((KW, per_piece, span, LANES), f32),
        ((nz, head_width, chunk_w), f32),
        ((nz, nf, half, chunk_w), bf16),
        ((nz, nf, half, chunk_w), bf16),
        ((nz, nf, half, chunk_w), bf16),
        ((nz, nf, half, chunk_w), bf16),
        ((half, chunk_w), f32),
        ((nz, half, chunk_w), bf16),
        ((nz, half, chunk_w), bf16),
        ((2, nz, half, chunk_w), bf16),
        ((nf, per_shard, KW, LANES), bf16),
        ((nf, per_shard, KW, LANES), bf16),
        ((per_shard, KW, LANES), bf16),
        ((nz, per_shard, KW, LANES), bf16),
        ((per_shard, KW, LANES), bf16),
        ((per_shard, KW, LANES), bf16),
    ]
    sems = [
        (6,), (2, 4), (2, 4), (nz, nf), (nz, nf), (nz, nf), (nz, nf), (nf,), (nf,), (nz,), (nz,), (nz, nf), (nz, nf),
        (nz,), (nz,), (nz,), (nz,), (nz,), (nz,), (nf,), (nf,), (nz,), (nz,),
    ]
    context_grad, weight_grad, kernel_grad = pl.pallas_call(
        functools.partial(block_kernel, nt, nf),
        out_shape=(
            jax.ShapeDtypeStruct((rows, head_width), bf16),
            jax.ShapeDtypeStruct((shard, width), f32),
            jax.ShapeDtypeStruct((KW, width // nf), f32),
        ),
        in_specs=[pl.BlockSpec(memory_space=pltpu.SMEM)] + [pl.BlockSpec(memory_space=pltpu.HBM)] * 6,
        out_specs=(vmem, vmem, vmem),
        scratch_shapes=[pltpu.VMEM(*s) for s in scratch]
        + [dma(s) for s in sems]
        + [dma, dma],
        compiler_params=pltpu.CompilerParams(
            collective_id=0, has_side_effects=True, vmem_limit_bytes=60 * 1024 * 1024
        ),
    )(utt_starts, queries[0], keys_values[0], inputs[0], cotangent[0], out_weight, conv_kernel)
    return (context_grad[None], weight_grad, kernel_grad)


def fits(nt, nf, queries, keys_values, inputs, cotangent, out_weight, conv_kernel, utt_starts):
    rows, head_width = queries.shape[1:]
    width = inputs.shape[2]
    return (
        queries.shape[0] == 1
        and rows == 2 * BLOCK
        and nt % 2 == 0
        and nt >= 4
        and (width // LANES) % (nt // 2) == 0
        and (width // LANES) % nf == 0
        and out_weight.shape[0] % 32 == 0
        and head_width * LANES == HEADS_W * 96 * LANES
    )


def solution(mesh):
    nt, nf = mesh.shape["tm"], mesh.shape["fsdp"]

    def body(*arrays):
        if fits(nt, nf, *arrays):
            return fused(nt, nf, *arrays)
        return shards(*arrays)

    return jax.shard_map(
        body,
        mesh=mesh,
        in_specs=(
            P("fsdp", "tm", None),
            P("fsdp", "tm", None),
            P("fsdp", "tm", None),
            P("fsdp", "tm", None),
            P("fsdp", None),
            P(None, "fsdp"),
            P("fsdp", None),
        ),
        out_specs=(P("fsdp", "tm", None), P("fsdp", None), P(None, "fsdp")),
        check_vma=False,
    )
```
